512 devices in a mesh: op: 128 (over y, z, core), blk: 4 (over x).
Axes of the slice: x: 4, y: 8, z: 8, core: 2. Of those that a mesh axis runs over, the one named last changes fastest.
Arguments:
- wavefunction: bfloat16 [2, 8, 384, 384], P(None, 'blk'), may hold values from -160 to 160
- left_ops: bfloat16 [512, 8, 384, 384], P('op', 'blk'), may hold values from -1.25 to 1.25
- right_ops: bfloat16 [512, 8, 384, 384], P('op', 'blk'), may hold values from -0.013671875 to 0.013671875
- shifts: int32 [512], P('op'), may hold values from -1 to 1
- sector_sizes: int32 [8], replicated, may hold values from 1 to 384, 2688 in all
- site_coef: float32 [128, 512], P('op'), may hold values from 0.25 to 4
- site_energy: float32 [128], P('op'), may hold values from -3 to -1
- site_owner: int32 [1], replicated, may hold values from 0 to 127
Outputs:
- residual: float32 [384, 2, 8, 384], P('op', None, 'blk')
- rayleigh: float32 [2], replicated
The draws below stay inside these ranges and needn't reach their ends.
Inputs may be any that keep to these rules, and one draw needn't show every extreme that they name: Left and right blocks of pair k map sector b - shifts[k] to sector b. `sector_sizes`: the sizes sum to 2688; the largest equals 384.
All inputs are finite; a program needn't handle non-finite values.
Results may differ from the reference program's by a relative error of at most 0.00055.
The reference program's roundings to bfloat16 on the way (of `psi_live` and `left_part`) count: a program that leaves them out, or rounds other values in their place, can miss the bound.
Values may be sent and summed in bfloat16 or wider, within the bound.
No kernel may reach another device: no remote copies, remote signals or barrier semaphores. Data moves between devices by JAX's collectives and lax.ppermute only.
A program may use at most 64 MiB of HBM per device.

```python
import math
import jax
import jax.numpy as jnp
import numpy as np
from jax import lax

SECT = 384
SECTORS = 8
NV = 2
NOPS = 512
BOND = 2688
N_OP = 128


def draw_wavefunction(key, part):
    key = jax.random.fold_in(key, 11)
    keys = jax.random.split(key, 3)
    shape = (NV, SECTORS, SECT, SECT)
    base = jnp.clip(jax.random.normal(keys[0], shape, jnp.float32), -3.0, 3.0)
    slope = 0.73
    row_scale = jnp.exp(jax.random.uniform(keys[1], (NV, SECTORS, SECT, 1), jnp.float32, -1.15, 1.15))
    col_scale = jnp.exp(jax.random.uniform(keys[2], (NV, SECTORS, 1, SECT), jnp.float32, -1.15, 1.15))
    position = jnp.arange(SECT, dtype=jnp.float32)[:, None] / SECT
    sector = jnp.arange(SECTORS, dtype=jnp.float32)[:, None, None] / SECTORS
    trend = (1.0 + slope * position) * (1.0 + slope * sector)
    return (base * row_scale * col_scale * trend[None]).astype(jnp.bfloat16)


def place_ends(entries, own_key, least, largest):
    longest = entries.shape.index(max(entries.shape))
    spots = []
    for shift in (0, 1):
        where = [jax.random.randint(jax.random.fold_in(own_key, axis), (), 0, length) for axis, length in enumerate(entries.shape)]
        where[longest] = (where[longest] + shift) % entries.shape[longest]
        spots.append(tuple(where))
    return entries.at[spots[0]].set(least).at[spots[1]].set(largest)


def raised(drawn, rng, source, target, blocks, factor):
    owner, partner = [(jnp.arange(drawn.shape[axis_at]) // (drawn.shape[axis_at] // blocks)).reshape([-1 if axis == axis_at else 1 for axis in range(drawn.ndim)]) for axis_at in (source, target)]
    chosen = jax.random.permutation(rng, blocks)[partner]
    strong = (owner == chosen) | (owner == (partner + blocks // 2) % blocks)
    return jnp.where(strong, factor * drawn, drawn)


def block_levels(own_key, dims, shards, smallest, largest):
    level, own = 1.0, jax.random.fold_in(own_key, 6)
    for dim, parts in shards:
        steps = jnp.exp(jax.random.uniform(jax.random.fold_in(own, dim), (parts,), jnp.float32, smallest / len(shards), largest / len(shards)))
        level = level * jnp.repeat(steps, dims[dim] // parts).reshape([-1 if axis == dim else 1 for axis in range(len(dims))])
    return level


def split_up(count, total, limit, skew):
    weights = [(1 << 20) // math.isqrt(rank ** skew) + 1 for rank in range(2, count + 1)]
    spare, counts = total - limit - (count - 1), [1] * (count - 1)
    while spare > 0:
        free = [i for i in range(count - 1) if counts[i] < limit]
        mass, left = sum([weights[i] for i in free]), spare
        for i in free:
            addition = min(limit - counts[i], max(1, left * weights[i] // mass), spare)
            counts[i] = counts[i] + addition
            spare = spare - addition
    return np.array([limit] + counts)


def uneven_parts(rng, number_of, total, reach, skew):
    if number_of == 2:
        one = jax.random.randint(rng, (), max(1, total - reach), min(reach, total - 1) + 1)
        return jnp.stack([one, total - one])
    lengths = jnp.asarray(split_up(number_of, total, reach, skew), jnp.int32)
    couples = (number_of - 1) // 2
    giver, taker = lengths[1:1 + 2 * couples:2], lengths[2:2 + 2 * couples:2]
    slack = jnp.minimum(giver - 1, reach - taker)
    shifted = jax.random.randint(jax.random.fold_in(rng, 1), (couples,), 0, 1 << 20) % (slack + 1)
    lengths = lengths.at[1:1 + 2 * couples:2].set(giver - shifted).at[2:2 + 2 * couples:2].set(taker + shifted)
    return lengths[jax.random.permutation(jax.random.fold_in(rng, 2), number_of)]


def scatter_about(stream_key, shape, deviation, limit, shards=(), kind=jnp.bfloat16):
    loudness = block_levels(stream_key, shape, shards, -0.22, 0.18) if shards else 1.0
    array = jax.random.normal(stream_key, shape, jnp.float32) * deviation * loudness
    return jnp.minimum(jnp.maximum(array, -limit), limit).astype(kind)


def bell_draw_with(key, dims, deviation, bound, cuts, heavy, kind=jnp.bfloat16):
    array = deviation * jax.random.normal(key, dims, jnp.float32)
    if cuts:
        array = array * block_levels(key, dims, cuts, -0.22, 0.18)
    return jnp.clip(raised(array, jax.random.fold_in(key, 3), *heavy), -bound, bound).astype(kind)


def setup_inputs(seed: int = 0) -> dict:
    key_of = jax.random.split(jax.random.key(seed), 9)
    return {
        "wavefunction": draw_wavefunction(jax.random.fold_in(key_of[8], 71), 0),
        "left_ops": bell_draw_with(key_of[1], (NOPS, SECTORS, SECT, SECT), SECT ** -0.5, 1.25, ((0, 128), (1, 4)), (0, 2, 128, 5.5)),
        "right_ops": scatter_about(key_of[2], (NOPS, SECTORS, SECT, SECT), (SECT * NOPS) ** -0.5, 0.013671875, ((0, 128), (1, 4))),
        "shifts": place_ends(jax.random.randint(key_of[3], (NOPS,), -1, 2), jax.random.fold_in(key_of[3], 1), -1, 1).astype(jnp.int32),
        "sector_sizes": uneven_parts(key_of[4], SECTORS, BOND, SECT, 1).astype(jnp.int32),
        "site_coef": jnp.clip(jnp.exp(math.log(4.0) - 2.7725887 * jax.random.uniform(key_of[5], (N_OP, NOPS), jnp.float32) ** block_levels(key_of[5], (N_OP, NOPS), ((0, 128),), -0.2, 0.2)), 0.25, 4.0),
        "site_energy": jnp.clip(-3.0 + 2.0 * jax.random.uniform(key_of[6], (N_OP,), jnp.float32) ** block_levels(key_of[6], (N_OP,), ((0, 128),), -0.2, 0.2), -3.0, -1.0),
        "site_owner": jax.random.randint(key_of[7], (1,), 0, N_OP).astype(jnp.int32),
    }


def live_masks(sector_sizes):
    row_ids = jnp.arange(SECT, dtype=jnp.int32)
    live_rows = row_ids[None, :] < sector_sizes[:, None]
    return live_rows[:, :, None] & live_rows[:, None, :]


def reference(wavefunction, left_ops, right_ops, shifts, sector_sizes, site_coef, site_energy, site_owner):
    live_mask = live_masks(sector_sizes)
    psi_live = jnp.where(live_mask[None], wavefunction, jnp.zeros((), wavefunction.dtype))
    padded = jnp.pad(psi_live, ((0, 0), (1, 1), (0, 0), (0, 0)))
    weights = site_coef[site_owner[0]]
    energy = site_energy[site_owner[0]]

    def add_pair(running, item):
        left, right, shift, weight = item
        source = lax.dynamic_slice_in_dim(padded, (1 - shift).astype(jnp.int32), SECTORS, 1)
        left_part = jnp.einsum("bis,vbsc->vbic", left.astype(jnp.float32), source.astype(jnp.float32),
                               precision=lax.Precision.HIGHEST).astype(jnp.bfloat16)
        full_term = jnp.einsum("vbic,bdc->vbid", left_part.astype(jnp.float32), right.astype(jnp.float32),
                               precision=lax.Precision.HIGHEST)
        return running + weight * full_term, None

    summed, _ = lax.scan(add_pair, jnp.zeros(wavefunction.shape, jnp.float32),
                         (left_ops, right_ops, shifts, weights))
    live_float = live_mask.astype(jnp.float32)
    psi_float = psi_live.astype(jnp.float32)
    sigma = live_float[None] * summed + energy * psi_float
    norm_sum = jnp.sum(psi_float * psi_float, axis=(1, 2, 3))
    correlation = jnp.sum(psi_float * sigma, axis=(1, 2, 3))
    rayleigh = correlation / (norm_sum + 1e-6)
    residual = sigma - rayleigh[:, None, None, None] * psi_float
    return jnp.transpose(residual, (2, 0, 1, 3)), rayleigh
```

```python
import functools

import jax
import jax.numpy as jnp
from jax import lax
from jax.experimental import pallas as pl
from jax.experimental.pallas import tpu as pltpu
from jax.sharding import Mesh, PartitionSpec as P

F32, F16, BF16 = jnp.float32, jnp.float16, jnp.bfloat16
OP = ("chip", "core")
SPLIT = 2048.0


def sigma_kernel(
    pairs, meta, weight, psi, halo, left_own, left_got, right_own, right_got, acc, stats, src
):
    step = pl.program_id(0)
    size = acc.shape[1]
    core = meta[2 * pairs + 3]

    @pl.when(step == 0)
    def _():
        row = lax.broadcasted_iota(jnp.int32, (size, size), 0)
        col = lax.broadcasted_iota(jnp.int32, (size, size), 1)
        for slot in range(3):
            live = jnp.maximum(row, col) < meta[2 * pairs + slot]
            for v in range(2):
                block = psi[v, slot] if slot < 2 else halo[v]
                src[slot, :, v * size : (v + 1) * size] = jnp.where(
                    live, block.astype(F32), 0.0
                ).astype(BF16)

    def add_pair(left, right):
        part = jnp.dot(left[...], src[meta[step]], preferred_element_type=F32).astype(BF16)
        for v in range(2):
            term = weight[step] * lax.dot_general(
                part[:, v * size : (v + 1) * size],
                right[...],
                (((1,), (1,)), ((), ())),
                preferred_element_type=F32,
            )

            @pl.when(step == 0)
            def _():
                acc[v] = term

            @pl.when(step > 0)
            def _():
                acc[v] += term

    @pl.when(step < pairs)
    def _():
        add_pair(left_own.at[0, 0], right_own.at[0, 0])

    @pl.when(step >= pairs)
    def _():
        add_pair(left_got.at[0], right_got.at[0])

    @pl.when(step == 2 * pairs - 1)
    def _():
        top = 0.0
        for v in range(2):
            own = src[core, :, v * size : (v + 1) * size].astype(F32)
            total = acc[v]
            stats[v] = jnp.sum(own * total)
            stats[2 + v] = jnp.sum(own * own)
            top = jnp.maximum(top, jnp.max(jnp.abs(total)))
        stats[4] = top


def sigma_partial(meta, weight, psi, halo, left, left_got, right, right_got):
    pairs, _, size, _ = left.shape
    own = pl.BlockSpec(
        (1, 1, size, size), lambda i, m, w: (jnp.minimum(i, pairs - 1), m[2 * pairs + 3], 0, 0)
    )
    got = pl.BlockSpec((1, size, size), lambda i, m, w: (jnp.maximum(i - pairs, 0), 0, 0))
    whole = lambda shape: pl.BlockSpec(shape, lambda i, m, w: (0,) * len(shape))
    return pl.pallas_call(
        functools.partial(sigma_kernel, pairs),
        grid_spec=pltpu.PrefetchScalarGridSpec(
            num_scalar_prefetch=2,
            grid=(2 * pairs,),
            in_specs=[whole(psi.shape), whole(halo.shape), own, got, own, got],
            out_specs=[whole((2, size, size)), pl.BlockSpec(memory_space=pltpu.SMEM)],
            scratch_shapes=[pltpu.VMEM((3, size, 2 * size), BF16)],
        ),
        out_shape=[
            jax.ShapeDtypeStruct((2, size, size), F32),
            jax.ShapeDtypeStruct((8,), F32),
        ],
        compiler_params=pltpu.CompilerParams(
            dimension_semantics=("arbitrary",), vmem_limit_bytes=40 * 1024 * 1024
        ),
        cost_estimate=pl.CostEstimate(
            flops=2 * pairs * 8 * size**3,
            bytes_accessed=2 * (4 * pairs + 6) * size * size + 8 * size * size,
            transcendentals=0,
        ),
        name="sigma_partial",
    )(meta, weight, psi, halo, left, left_got, right, right_got)


def power_above(value, head):
    return jnp.maximum(jnp.ceil(jnp.log2(jnp.maximum(value, 1e-30))), -90.0) - head


def on_device(
    wavefunction, left_ops, right_ops, shifts, sector_sizes, site_coef, site_energy, site_owner
):
    vectors, _, size, _ = wavefunction.shape
    pairs = left_ops.shape[0]
    sectors = sector_sizes.shape[0]
    chips, blks = lax.axis_size("chip"), lax.axis_size("blk")
    chip, core, blk = lax.axis_index("chip"), lax.axis_index("core"), lax.axis_index("blk")
    other = 1 - core
    op = chip * 2 + core
    chip_rows = size // chips
    rows = chip_rows // 2

    swap = [(0, 1), (1, 0)]
    take = lambda array, index: lax.dynamic_index_in_dim(array, index, 1, keepdims=False)
    halo_path = [(x, x + 1) for x in range(blks - 1)] + [
        (blks + x + 1, blks + x) for x in range(blks - 1)
    ]
    halo = lax.ppermute(take(wavefunction, other), ("core", "blk"), halo_path)
    left_got = lax.ppermute(take(left_ops, other), "core", swap)
    right_got = lax.ppermute(take(right_ops, other), "core", swap)

    words = jnp.concatenate(
        [
            jnp.repeat(site_coef.reshape(chips, 2 * pairs), 2, axis=0),
            jnp.broadcast_to(
                jnp.concatenate([site_energy, shifts.astype(F32)])[None], (2 * chips, 1 + pairs)
            ),
        ],
        axis=1,
    )
    words = lax.all_to_all(words, OP, 0, 0, tiled=True)
    owned = lax.dynamic_index_in_dim(words, site_owner[0], 0, keepdims=False)
    energy = owned[2 * pairs]
    shifts_got = lax.dynamic_slice(words, (chip * 2 + other, 2 * pairs + 1), (1, pairs))[0]
    chip_weights = owned[: 2 * pairs].reshape(2, pairs)
    weights = jnp.where(core == 0, chip_weights, chip_weights[::-1]).reshape(-1)
    place = core - jnp.concatenate([shifts, jnp.round(shifts_got).astype(jnp.int32)])
    slots = jnp.where((place == 0) | (place == 1), place, 2)
    far = 2 * blk - 1 + 3 * core
    ids = jnp.stack([2 * blk, 2 * blk + 1, far])
    sizes = jnp.where(
        (ids >= 0) & (ids < sectors), sector_sizes[jnp.clip(ids, 0, sectors - 1)], 0
    )
    meta = jnp.concatenate([slots, sizes, core[None]]).astype(jnp.int32)
    partial, stats = sigma_partial(
        meta, weights, wavefunction, halo, left_ops, left_got, right_ops, right_got
    )

    level = power_above(stats[4], 14.0)
    cross = stats[:2]
    cross_level = power_above(jnp.max(jnp.abs(cross)), 0.0)
    value = cross * jnp.exp2(-cross_level)
    pieces = []
    for _ in range(3):
        piece = value.astype(F16)
        pieces.append(piece)
        value = (value - piece.astype(F32)) * SPLIT
    tags = jnp.concatenate([jnp.stack([level, cross_level]).astype(F16)] + pieces)
    blocks = (partial * jnp.exp2(-level)).astype(F16)
    blocks = blocks.reshape(vectors, chips, chip_rows, size).transpose(1, 0, 2, 3)
    lines = vectors * chip_rows * size // 128
    blocks = jnp.concatenate(
        [
            blocks.reshape(chips, lines, 128),
            jnp.broadcast_to(jnp.pad(tags, (0, 120))[None, None], (chips, 1, 128)),
            jnp.zeros((chips, -(lines + 1) % 8, 128), F16),
        ],
        axis=1,
    )
    blocks = lax.all_to_all(blocks, "chip", 0, 0, tiled=True)
    tags = blocks[:, lines, :8].astype(F32)
    cross = jnp.sum(
        (tags[:, 2:4] + (tags[:, 4:6] + tags[:, 6:8] / SPLIT) / SPLIT) * jnp.exp2(tags[:, 1:2]),
        axis=0,
    )
    summed = jnp.sum(
        blocks[:, :lines].astype(F32) * jnp.exp2(tags[:, 0])[:, None, None], axis=0
    ).reshape(vectors, 2, rows, size)

    got = lax.ppermute(take(summed, other), "core", swap)
    kept = take(summed, core)
    ours = jnp.where(core == 0, jnp.stack([kept, got], 2), jnp.stack([got, kept], 2))
    sums = jnp.broadcast_to(jnp.concatenate([cross, stats[2:4]])[None], (2 * blks, 4))
    sums = jnp.sum(lax.all_to_all(sums, ("core", "blk"), 0, 0, tiled=True), axis=0)
    cross_sum, norm_sum = sums[:2], sums[2:]
    rayleigh = (cross_sum + energy * norm_sum) / (norm_sum + 1e-06)

    first = op * rows
    own_sizes = lax.dynamic_slice_in_dim(sector_sizes, 2 * blk, 2, 0)[:, None, None]
    row_ids = first + jnp.arange(rows, dtype=jnp.int32)[None, :, None]
    col_ids = jnp.arange(size, dtype=jnp.int32)[None, None, :]
    live = ((row_ids < own_sizes) & (col_ids < own_sizes)).transpose(1, 0, 2)[:, None]
    psi_rows = lax.dynamic_slice_in_dim(wavefunction, first, rows, 2)
    psi_rows = psi_rows.transpose(2, 0, 1, 3).astype(F32)
    value = ours.transpose(1, 0, 2, 3) + (energy - rayleigh)[None, :, None, None] * psi_rows
    return jnp.where(live, value, 0.0), rayleigh


def solution(mesh):
    ops, blks = mesh.devices.shape
    split = Mesh(mesh.devices.reshape(ops // 2, 2, blks), OP + ("blk",))
    return jax.shard_map(
        on_device,
        mesh=split,
        in_specs=(
            P(None, "blk", None, None),
            P(OP, "blk", None, None),
            P(OP, "blk", None, None),
            P(OP),
            P(),
            P(OP, None),
            P(OP),
            P(),
        ),
        out_specs=(P(OP, None, "blk", None), P()),
        check_vma=False,
    )
```

```python
import functools

import jax
import jax.numpy as jnp
from jax import lax
from jax.experimental import pallas as pl
from jax.experimental.pallas import tpu as pltpu
from jax.sharding import Mesh, PartitionSpec as P

F32, F16, BF16 = jnp.float32, jnp.float16, jnp.bfloat16
OP = ("chip", "core")
HEAD, PIECE = 1024.0, 2048.0
TILES = 4
LANES = 128
SMEM = pl.BlockSpec(memory_space=pltpu.SMEM)
VMEM = pl.BlockSpec(memory_space=pltpu.VMEM)
ANY = pl.BlockSpec(memory_space=pl.ANY)


def products(core, shifts, src, left, right, terms, lefts, rights, sems):
    pairs, size = lefts.shape[0], lefts.shape[1]
    for k in range(pairs):
        pltpu.make_async_copy(left.at[k, core], lefts.at[k], sems.at[0, k]).wait()
        slot = core - shifts[k]
        slot = jnp.where((slot == 0) | (slot == 1), slot, 2)
        part = jnp.dot(lefts[k], src[slot], preferred_element_type=F32).astype(BF16)
        pltpu.make_async_copy(right.at[k, core], rights.at[k], sems.at[1, k]).wait()
        for v in range(2):
            terms[k, v] = lax.dot_general(
                part[:, v * size : (v + 1) * size],
                rights[k],
                (((1,), (1,)), ((), ())),
                preferred_element_type=F32,
            )


def start_loads(core, left, right, lefts, rights, sems):
    for k in range(lefts.shape[0]):
        pltpu.make_async_copy(left.at[k, core], lefts.at[k], sems.at[0, k]).start()
        pltpu.make_async_copy(right.at[k, core], rights.at[k], sems.at[1, k]).start()


def own_kernel(
    place, shifts, sizes, psi, halo, left, right, terms, src, psis, halos, lefts, rights, sems, more
):
    core, blk = place[0], place[1]
    psi_copy = pltpu.make_async_copy(psi, psis, more.at[0])
    halo_copy = pltpu.make_async_copy(halo, halos, more.at[1])
    psi_copy.start()
    halo_copy.start()
    start_loads(core, left, right, lefts, rights, sems)
    size = psis.shape[2]
    row = lax.broadcasted_iota(jnp.int32, (size, size), 0)
    col = lax.broadcasted_iota(jnp.int32, (size, size), 1)
    reach = jnp.maximum(row, col)
    far = 2 * blk - 1 + 3 * core
    inside = (far >= 0) & (far < sizes.shape[0])
    far_size = jnp.where(inside, sizes[jnp.clip(far, 0, sizes.shape[0] - 1)], 0)
    for slot, live_size in enumerate((sizes[2 * blk], sizes[2 * blk + 1], far_size)):
        if slot == 0:
            psi_copy.wait()
        if slot == 2:
            halo_copy.wait()
        live = jnp.where(reach < live_size, 1.0, 0.0).astype(BF16)
        for v in range(2):
            block = psis[v, slot] if slot < 2 else halos[v]
            src[slot, :, v * size : (v + 1) * size] = block * live
    products(core, shifts, src, left, right, terms, lefts, rights, sems)


def got_kernel(place, shifts, src, left, right, terms, lefts, rights, sems):
    core = place[0]
    start_loads(core, left, right, lefts, rights, sems)
    products(core, shifts, src, left, right, terms, lefts, rights, sems)


def estimate(pairs, size):
    return pl.CostEstimate(
        flops=8 * pairs * size**3, bytes_accessed=20 * pairs * size * size, transcendentals=0
    )


def load_scratch(pairs, size):
    return [
        pltpu.VMEM((pairs, size, size), BF16),
        pltpu.VMEM((pairs, size, size), BF16),
        pltpu.SemaphoreType.DMA((2, pairs)),
    ]


def own_terms(place, shifts, sizes, psi, halo, left, right):
    pairs, _, size, _ = left.shape
    return pl.pallas_call(
        own_kernel,
        in_specs=[SMEM] * 3 + [ANY] * 4,
        out_specs=[VMEM, VMEM],
        out_shape=[
            jax.ShapeDtypeStruct((pairs, 2, size, size), F32),
            jax.ShapeDtypeStruct((3, size, 2 * size), BF16),
        ],
        scratch_shapes=[pltpu.VMEM(psi.shape, BF16), pltpu.VMEM(halo.shape, BF16)]
        + load_scratch(pairs, size)
        + [pltpu.SemaphoreType.DMA((2,))],
        compiler_params=pltpu.CompilerParams(vmem_limit_bytes=32 * 1024 * 1024),
        cost_estimate=estimate(pairs, size),
        name="own_terms",
    )(place, shifts, sizes, psi, halo, left, right)


def got_terms(place, shifts, src, left, right):
    pairs, _, size, _ = left.shape
    return pl.pallas_call(
        got_kernel,
        in_specs=[SMEM] * 2 + [VMEM] + [ANY] * 2,
        out_specs=VMEM,
        out_shape=jax.ShapeDtypeStruct((pairs, 2, size, size), F32),
        scratch_shapes=load_scratch(pairs, size),
        compiler_params=pltpu.CompilerParams(vmem_limit_bytes=32 * 1024 * 1024),
        cost_estimate=estimate(pairs, size),
        name="got_terms",
    )(place, shifts, src, left, right)


def level_of(top, head):
    return jnp.maximum(jnp.ceil(jnp.log2(jnp.maximum(top, 1e-30))), -90.0) - head


def folded(values):
    rows, columns = values.shape
    total = None
    for r in range(0, rows, 8):
        for c in range(0, columns, LANES):
            part = values[r : r + 8, c : c + LANES]
            total = part if total is None else total + part
    return total


def combine_kernel(chip_rows, place, owner, words, own, got, src, packed, norm, sums):
    step = pl.program_id(0)
    pairs, _, rows, size = own.shape
    core, chip = place[0], place[2]
    here = rows // chip_rows
    parts = size // LANES
    tag = 2 * parts * chip_rows
    tagged = packed.shape[1] - tag
    line = jnp.broadcast_to(words[owner[0], 0:1, :], (8, LANES))
    first = lax.rem(chip * 2 * pairs, LANES)
    own_weight = pltpu.roll(line, LANES - first - core * pairs, 1)
    got_weight = pltpu.roll(line, LANES - first - (1 - core) * pairs, 1)

    @pl.when(step == 0)
    def _():
        sums[...] = jnp.zeros_like(sums)

    totals = []
    for v in range(2):
        total = own_weight[0:1, 0:1] * own[0, v]
        for k in range(1, pairs):
            total += own_weight[0:1, k : k + 1] * own[k, v]
        for k in range(pairs):
            total += got_weight[0:1, k : k + 1] * got[k, v]
        psi = src[0, :, v * size : (v + 1) * size].astype(F32)
        sums[v] += folded(psi * total)
        sums[2 + v] += folded(psi * psi)
        totals.append(total)
    top = jnp.max(jnp.maximum(jnp.abs(totals[0]), jnp.abs(totals[1])), keepdims=True)
    level = level_of(top, 14.0)
    scale = jnp.exp2(-level)
    row = lax.broadcasted_iota(jnp.int32, (tagged, LANES), 0)
    lane = lax.broadcasted_iota(jnp.int32, (tagged, LANES), 1)
    mark = jnp.where(row == 0, level, 0.0)
    for v in range(2):
        scaled = totals[v] * scale
        for j in range(here):
            for t in range(parts):
                at = (v * parts + t) * chip_rows
                packed[step * here + j, at : at + chip_rows, :] = scaled[
                    j * chip_rows : (j + 1) * chip_rows, t * LANES : (t + 1) * LANES
                ]
    for j in range(here):
        packed[step * here + j, tag:, :] = mark

    @pl.when(step == pl.num_programs(0) - 1)
    def _():
        cross = [jnp.sum(sums[v], keepdims=True) for v in range(2)]
        level = level_of(jnp.maximum(jnp.abs(cross[0]), jnp.abs(cross[1])), 0.0)
        values = [level]
        rest = [value * jnp.exp2(-level) * HEAD for value in cross]
        for _ in range(3):
            heads = [jnp.round(value) for value in rest]
            values += heads
            rest = [(value - head) * PIECE for value, head in zip(rest, heads)]
        tags = jnp.zeros((tagged, LANES), F32)
        for i, value in enumerate(values):
            tags = jnp.where((row == 0) & (lane == i + 1), value, tags)
        for j in range(packed.shape[0]):
            packed[j, tag:, :] = jnp.where(lane == 0, packed[j, tag:, :], tags)
        for v in range(2):
            norm[v : v + 1, :] = jnp.broadcast_to(jnp.sum(sums[2 + v], keepdims=True), (1, LANES))


def combined(chips, place, owner, words, own, got, src):
    pairs, _, size, _ = own.shape
    chip_rows = size // chips
    tile = size // TILES
    lines = -(-(2 * chip_rows * size // LANES + 1) // 8) * 8
    whole = lambda shape: pl.BlockSpec(shape, lambda i, p, o: (0,) * len(shape))
    terms = pl.BlockSpec((pairs, 2, tile, size), lambda i, p, o: (0, 0, i, 0))
    return pl.pallas_call(
        functools.partial(combine_kernel, chip_rows),
        grid_spec=pltpu.PrefetchScalarGridSpec(
            num_scalar_prefetch=2,
            grid=(TILES,),
            in_specs=[
                whole(words.shape),
                terms,
                terms,
                pl.BlockSpec((1, tile, 2 * size), lambda i, p, o: (p[0], i, 0)),
            ],
            out_specs=[whole((chips, lines, LANES)), whole((2, LANES))],
            scratch_shapes=[pltpu.VMEM((4, 8, LANES), F32)],
        ),
        out_shape=[
            jax.ShapeDtypeStruct((chips, lines, LANES), F32),
            jax.ShapeDtypeStruct((2, LANES), F32),
        ],
        compiler_params=pltpu.CompilerParams(vmem_limit_bytes=32 * 1024 * 1024),
        name="combined",
    )(place, owner, words, own, got, src)


def on_device(
    wavefunction, left_ops, right_ops, shifts, sector_sizes, site_coef, site_energy, site_owner
):
    size = wavefunction.shape[2]
    pairs = left_ops.shape[0]
    chips, blks = lax.axis_size("chip"), lax.axis_size("blk")
    chip, core, blk = lax.axis_index("chip"), lax.axis_index("core"), lax.axis_index("blk")
    chip_rows = size // chips
    rows = chip_rows // 2
    parts = size // LANES
    place = jnp.stack([core, blk, chip]).astype(jnp.int32)

    swap = [(0, 1), (1, 0)]
    halo_path = [(x, x + 1) for x in range(blks - 1)] + [
        (blks + x + 1, blks + x) for x in range(blks - 1)
    ]
    edge = lax.dynamic_index_in_dim(wavefunction, 1 - core, 1, keepdims=False)
    halo = lax.ppermute(edge, ("core", "blk"), halo_path)
    lines = site_coef.reshape(-1, 1, LANES)
    lines = jnp.broadcast_to(lines, (lines.shape[0], 2 * chips // lines.shape[0], LANES))
    words = jnp.stack(
        [lines.reshape(2 * chips, LANES), jnp.broadcast_to(site_energy[:, None], (2 * chips, LANES))],
        axis=1,
    )
    words = lax.all_to_all(words, OP, 0, 0, tiled=True)
    left_got = lax.ppermute(left_ops, "core", swap)
    right_got = lax.ppermute(right_ops, "core", swap)
    shifts_got = lax.ppermute(shifts, "core", swap)

    own, src = own_terms(place, shifts, sector_sizes, wavefunction, halo, left_ops, right_ops)
    got = got_terms(place, shifts_got, src, left_got, right_got)
    packed, norm = combined(chips, place, site_owner, words, own, got, src)

    blocks = lax.all_to_all(packed.astype(F16), "chip", 0, 0, tiled=True)
    tag = 2 * parts * chip_rows
    tags = blocks[:, tag, :8].astype(F32)
    cross = jnp.sum(
        (tags[:, 2:4] + (tags[:, 4:6] + tags[:, 6:8] / PIECE) / PIECE)
        / HEAD
        * jnp.exp2(tags[:, 1:2]),
        axis=0,
    )
    summed = jnp.sum(blocks[:, :tag].astype(F32) * jnp.exp2(tags[:, 0])[:, None, None], axis=0)

    halves = summed.reshape(2 * parts, 2, rows, LANES).transpose(1, 0, 2, 3)
    halves = halves.reshape(2, 1, 2 * parts * rows, LANES)
    halves = jnp.broadcast_to(halves, (2, blks) + halves.shape[2:])
    sums = jnp.pad(jnp.concatenate([cross, norm[:, 0]]), (0, LANES - 4))
    sums = jnp.broadcast_to(sums[None, None, None], (2, blks, 1, LANES))
    sent = jnp.concatenate([halves, sums], axis=2).reshape(2 * blks, -1, LANES)
    came = lax.all_to_all(sent, ("core", "blk"), 0, 0, tiled=True)
    sums = jnp.sum(came[:, -1, :4], axis=0)
    energy = lax.dynamic_index_in_dim(words[:, 1, 0], site_owner[0], 0, keepdims=False)
    cross_sum, norm_sum = sums[:2], sums[2:]
    rayleigh = (cross_sum + energy * norm_sum) / (norm_sum + 1e-06)
    ours = lax.dynamic_index_in_dim(came.reshape(2, blks, -1, LANES), blk, 1, keepdims=False)
    ours = ours[:, :-1].reshape(2, 2, parts, rows, LANES).transpose(3, 1, 0, 2, 4)
    ours = ours.reshape(rows, 2, 2, size)

    first = (chip * 2 + core) * rows
    own_sizes = lax.dynamic_slice_in_dim(sector_sizes, 2 * blk, 2, 0)[:, None]
    row_ids = (first + jnp.arange(rows, dtype=jnp.int32))[:, None, None, None]
    col_ids = jnp.arange(size, dtype=jnp.int32)
    live = (row_ids < own_sizes) & (col_ids < own_sizes)
    psi_rows = lax.dynamic_slice_in_dim(wavefunction, first, rows, 2)
    psi_rows = psi_rows.transpose(2, 0, 1, 3).astype(F32)
    value = ours + (energy - rayleigh)[None, :, None, None] * psi_rows
    return jnp.where(live, value, 0.0), rayleigh


def solution(mesh):
    ops, blks = mesh.devices.shape
    split = Mesh(mesh.devices.reshape(ops // 2, 2, blks), OP + ("blk",))
    return jax.shard_map(
        on_device,
        mesh=split,
        in_specs=(
            P(None, "blk", None, None),
            P(OP, "blk", None, None),
            P(OP, "blk", None, None),
            P(OP),
            P(),
            P(OP, None),
            P(OP),
            P(),
        ),
        out_specs=(P(OP, None, "blk", None), P()),
        check_vma=False,
    )
```

```python
import functools

import jax
import jax.numpy as jnp
from jax import lax
from jax.experimental import pallas as pl
from jax.experimental.pallas import tpu as pltpu
from jax.sharding import Mesh, PartitionSpec as P

F32, F16, BF16 = jnp.float32, jnp.float16, jnp.bfloat16
OP = ("chip", "core")
HEAD, PIECE = 1024.0, 2048.0
TILES = 4
LANES = 128
SMEM = pl.BlockSpec(memory_space=pltpu.SMEM)
VMEM = pl.BlockSpec(memory_space=pltpu.VMEM)
HBM = pl.BlockSpec(memory_space=pltpu.HBM)
CORE, BLK, CHIP, SHIFTS = 0, 1, 2, 3


def loads(core, left, right, lefts, rights, sems):
    return [
        (
            pltpu.make_async_copy(left.at[k, core], lefts.at[k], sems.at[0, k]),
            pltpu.make_async_copy(right.at[k, core], rights.at[k], sems.at[1, k]),
        )
        for k in range(lefts.shape[0])
    ]


def product(core, shift, src, left, right, copies):
    size = left.shape[0]
    copies[0].wait()
    slot = core - shift
    slot = jnp.where((slot == 0) | (slot == 1), slot, 2)
    part = jnp.dot(left[...], src[slot], preferred_element_type=F32).astype(BF16)
    copies[1].wait()
    return [
        lax.dot_general(
            part[:, v * size : (v + 1) * size],
            right[...],
            (((1,), (1,)), ((), ())),
            preferred_element_type=F32,
        )
        for v in range(2)
    ]


def own_kernel(
    sectors, table, psi, halo, left, right, left_got, right_got, terms, sources,
    psis, halos, lefts, rights, made, src, sems, out_sems, more,
):
    core, blk = table[CORE], table[BLK]
    pairs, size = lefts.shape[0], lefts.shape[1]
    psi_copy = pltpu.make_async_copy(psi, psis, more.at[0])
    halo_copy = pltpu.make_async_copy(halo, halos, more.at[1])
    psi_copy.start()
    halo_copy.start()
    copies = loads(core, left, right, lefts, rights, sems)
    for pair in copies:
        for copy in pair:
            copy.start()
    row = lax.broadcasted_iota(jnp.int32, (size, size), 0)
    col = lax.broadcasted_iota(jnp.int32, (size, size), 1)
    reach = jnp.maximum(row, col)
    sizes = SHIFTS + pairs
    far = 2 * blk - 1 + 3 * core
    inside = (far >= 0) & (far < sectors)
    far_size = jnp.where(inside, table[sizes + jnp.clip(far, 0, sectors - 1)], 0)
    live_sizes = (table[sizes + 2 * blk], table[sizes + 2 * blk + 1], far_size)
    psi_copy.wait()
    halo_copy.wait()
    for slot, live_size in enumerate(live_sizes):
        live = jnp.where(reach < live_size, 1.0, 0.0).astype(BF16)
        for v in range(2):
            block = psis[v, slot] if slot < 2 else halos[v]
            src[slot, :, v * size : (v + 1) * size] = block * live
    source_copy = pltpu.make_async_copy(src, sources, more.at[2])
    source_copy.start()
    outs = []
    for k in range(pairs):
        terms_k = product(core, table[SHIFTS + k], src, lefts.at[k], rights.at[k], copies[k])
        for v in range(2):
            made[k, v] = terms_k[v]
        outs.append(pltpu.make_async_copy(made.at[k], terms.at[k], out_sems.at[k]))
        outs[k].start()
    source_copy.wait()
    for out in outs:
        out.wait()


def estimate(pairs, size):
    return pl.CostEstimate(
        flops=8 * pairs * size**3, bytes_accessed=20 * pairs * size * size, transcendentals=0
    )


def own_terms(sectors, table, psi, halo, left, right, left_got, right_got):
    pairs, _, size, _ = left.shape
    return pl.pallas_call(
        functools.partial(own_kernel, sectors),
        in_specs=[SMEM] + [HBM] * 6,
        out_specs=[HBM, HBM],
        out_shape=[
            jax.ShapeDtypeStruct((pairs, 2, size, size), F32),
            jax.ShapeDtypeStruct((3, size, 2 * size), BF16),
        ],
        scratch_shapes=[
            pltpu.VMEM(psi.shape, BF16),
            pltpu.VMEM(halo.shape, BF16),
            pltpu.VMEM((pairs, size, size), BF16),
            pltpu.VMEM((pairs, size, size), BF16),
            pltpu.VMEM((pairs, 2, size, size), F32),
            pltpu.VMEM((3, size, 2 * size), BF16),
            pltpu.SemaphoreType.DMA((2, pairs)),
            pltpu.SemaphoreType.DMA((pairs,)),
            pltpu.SemaphoreType.DMA((3,)),
        ],
        compiler_params=pltpu.CompilerParams(vmem_limit_bytes=62_850_000),
        cost_estimate=estimate(pairs, size),
        name="own_terms",
    )(table, psi, halo, left, right, left_got, right_got)


def level_of(top, head):
    return jnp.maximum(jnp.ceil(jnp.log2(jnp.maximum(top, 1e-30))), -90.0) - head


def folded(values):
    rows, columns = values.shape
    total = None
    for r in range(0, rows, 8):
        for c in range(0, columns, LANES):
            part = values[r : r + 8, c : c + LANES]
            total = part if total is None else total + part
    return total


def sigma_kernel(
    table, owner, words, own, sources, left, right, packed, norm,
    lefts, rights, owns, src, acc, sems, own_sems, more,
):
    core, chip = table[CORE], table[CHIP]
    pairs, size = lefts.shape[0], lefts.shape[1]
    source_copy = pltpu.make_async_copy(sources, src, more.at[0])
    source_copy.start()
    copies = loads(core, left, right, lefts, rights, sems)
    own_copies = [
        pltpu.make_async_copy(own.at[k], owns.at[k], own_sems.at[k]) for k in range(pairs)
    ]
    for k in range(pairs):
        copies[k][0].start()
        copies[k][1].start()
        own_copies[k].start()

    chips = packed.shape[0]
    chip_rows = size // chips
    parts = size // LANES
    tag = 2 * parts * chip_rows
    tagged = packed.shape[1] - tag
    line = jnp.broadcast_to(words[owner[0], 0:1, :], (8, LANES))
    first = lax.rem(chip * 2 * pairs, LANES)
    own_weight = pltpu.roll(line, LANES - first - core * pairs, 1)
    got_weight = pltpu.roll(line, LANES - first - (1 - core) * pairs, 1)
    facts = words[2 * chip + 1 - core, 1:2, :]
    spot = lax.broadcasted_iota(jnp.int32, (1, LANES), 1)
    shifts = [
        jnp.sum(jnp.where(spot == 1 + k, facts, 0.0)).astype(jnp.int32) for k in range(pairs)
    ]

    source_copy.wait()
    for k in range(pairs):
        terms = product(core, shifts[k], src, lefts.at[k], rights.at[k], copies[k])
        own_copies[k].wait()
        for v in range(2):
            total = got_weight[0:1, k : k + 1] * terms[v] + own_weight[0:1, k : k + 1] * owns[k, v]
            acc[v] = total if k == 0 else acc[v] + total

    tile = size // TILES
    here = chips // TILES
    row = lax.broadcasted_iota(jnp.int32, (tagged, LANES), 0)
    lane = lax.broadcasted_iota(jnp.int32, (tagged, LANES), 1)
    sums = [None] * 4
    for step in range(TILES):
        rows = slice(step * tile, (step + 1) * tile)
        top = None
        for v in range(2):
            total = acc[v, rows, :]
            psi = src[core, rows, v * size : (v + 1) * size].astype(F32)
            for i, part in ((v, folded(psi * total)), (2 + v, folded(psi * psi))):
                sums[i] = part if sums[i] is None else sums[i] + part
            high = jnp.max(jnp.abs(total), keepdims=True)
            top = high if top is None else jnp.maximum(top, high)
        level = level_of(top, 14.0)
        scale = jnp.exp2(-level)
        mark = jnp.where(row == 0, level, 0.0)
        for v in range(2):
            for j in range(here):
                chip_at = step * here + j
                for t in range(parts):
                    at = (v * parts + t) * chip_rows
                    packed[chip_at, at : at + chip_rows, :] = scale * acc[
                        v, chip_at * chip_rows : (chip_at + 1) * chip_rows, t * LANES : (t + 1) * LANES
                    ]
        for j in range(here):
            packed[step * here + j, tag:, :] = mark

    cross = [jnp.sum(sums[v], keepdims=True) for v in range(2)]
    level = level_of(jnp.maximum(jnp.abs(cross[0]), jnp.abs(cross[1])), 0.0)
    values = [level]
    rest = [value * jnp.exp2(-level) * HEAD for value in cross]
    for _ in range(3):
        heads = [jnp.round(value) for value in rest]
        values += heads
        rest = [(value - head) * PIECE for value, head in zip(rest, heads)]
    tags = jnp.zeros((tagged, LANES), F32)
    for i, value in enumerate(values):
        tags = jnp.where((row == 0) & (lane == i + 1), value, tags)
    for j in range(chips):
        packed[j, tag:, :] = jnp.where(lane == 0, packed[j, tag:, :], tags)
    for v in range(2):
        norm[v : v + 1, :] = jnp.broadcast_to(jnp.sum(sums[2 + v], keepdims=True), (1, LANES))


def sigma_blocks(chips, table, owner, words, own, sources, left, right):
    pairs, _, size, _ = left.shape
    lines = -(-(2 * size * size // chips // LANES + 1) // 8) * 8
    return pl.pallas_call(
        sigma_kernel,
        in_specs=[SMEM] * 2 + [VMEM] + [HBM] * 4,
        out_specs=[VMEM, VMEM],
        out_shape=[
            jax.ShapeDtypeStruct((chips, lines, LANES), F32),
            jax.ShapeDtypeStruct((2, LANES), F32),
        ],
        scratch_shapes=[
            pltpu.VMEM((pairs, size, size), BF16),
            pltpu.VMEM((pairs, size, size), BF16),
            pltpu.VMEM((pairs, 2, size, size), F32),
            pltpu.VMEM((3, size, 2 * size), BF16),
            pltpu.VMEM((2, size, size), F32),
            pltpu.SemaphoreType.DMA((2, pairs)),
            pltpu.SemaphoreType.DMA((pairs,)),
            pltpu.SemaphoreType.DMA((1,)),
        ],
        compiler_params=pltpu.CompilerParams(vmem_limit_bytes=61_880_000),
        cost_estimate=estimate(pairs, size),
        name="sigma_blocks",
    )(table, owner, words, own, sources, left, right)


def on_device(
    wavefunction, left_ops, right_ops, shifts, sector_sizes, site_coef, site_energy, site_owner
):
    size = wavefunction.shape[2]
    pairs = left_ops.shape[0]
    chips, blks = lax.axis_size("chip"), lax.axis_size("blk")
    chip, core, blk = lax.axis_index("chip"), lax.axis_index("core"), lax.axis_index("blk")
    chip_rows = size // chips
    rows = chip_rows // 2
    parts = size // LANES
    table = jnp.concatenate(
        [jnp.stack([core, blk, chip]).astype(jnp.int32), shifts, sector_sizes]
    )

    swap = [(0, 1), (1, 0)]
    halo_path = [(x, x + 1) for x in range(blks - 1)] + [
        (blks + x + 1, blks + x) for x in range(blks - 1)
    ]
    edge = lax.dynamic_index_in_dim(wavefunction, 1 - core, 1, keepdims=False)
    halo = lax.ppermute(edge, ("core", "blk"), halo_path)
    lines = site_coef.reshape(-1, 1, LANES)
    lines = jnp.broadcast_to(lines, (lines.shape[0], 2 * chips // lines.shape[0], LANES))
    facts = jnp.concatenate([site_energy, shifts.astype(F32)])
    facts = jnp.pad(facts, (0, LANES - 1 - pairs))
    words = jnp.stack(
        [lines.reshape(2 * chips, LANES), jnp.broadcast_to(facts, (2 * chips, LANES))], axis=1
    )
    words = lax.all_to_all(words, OP, 0, 0, tiled=True)
    left_got = lax.ppermute(left_ops, "core", swap)
    right_got = lax.ppermute(right_ops, "core", swap)
    own, sources = own_terms(
        sector_sizes.shape[0],
        table,
        wavefunction,
        halo,
        left_ops,
        right_ops,
        left_got,
        right_got,
    )
    packed, norm = sigma_blocks(
        chips, table, site_owner, words, own, sources, left_got, right_got
    )

    blocks = lax.all_to_all(packed.astype(F16), "chip", 0, 0, tiled=True)
    tag = 2 * parts * chip_rows
    tags = blocks[:, tag, :8].astype(F32)
    cross = jnp.sum(
        (tags[:, 2:4] + (tags[:, 4:6] + tags[:, 6:8] / PIECE) / PIECE)
        / HEAD
        * jnp.exp2(tags[:, 1:2]),
        axis=0,
    )
    summed = jnp.sum(blocks[:, :tag].astype(F32) * jnp.exp2(tags[:, 0])[:, None, None], axis=0)

    halves = summed.reshape(2 * parts, 2, rows, LANES).transpose(1, 0, 2, 3)
    halves = halves.reshape(2, 1, 2 * parts * rows, LANES)
    halves = jnp.broadcast_to(halves, (2, blks) + halves.shape[2:])
    sums = jnp.pad(jnp.concatenate([cross, norm[:, 0]]), (0, LANES - 4))
    sums = jnp.broadcast_to(sums[None, None, None], (2, blks, 1, LANES))
    sent = jnp.concatenate([halves, sums], axis=2).reshape(2 * blks, -1, LANES)
    came = lax.all_to_all(sent, ("core", "blk"), 0, 0, tiled=True)
    sums = jnp.sum(came[:, -1, :4], axis=0)
    energy = lax.dynamic_index_in_dim(words[:, 1, 0], site_owner[0], 0, keepdims=False)
    cross_sum, norm_sum = sums[:2], sums[2:]
    rayleigh = (cross_sum + energy * norm_sum) / (norm_sum + 1e-06)
    ours = lax.dynamic_index_in_dim(came.reshape(2, blks, -1, LANES), blk, 1, keepdims=False)
    ours = ours[:, :-1].reshape(2, 2, parts, rows, LANES).transpose(3, 1, 0, 2, 4)
    ours = ours.reshape(rows, 2, 2, size)

    first = (chip * 2 + core) * rows
    own_sizes = lax.dynamic_slice_in_dim(sector_sizes, 2 * blk, 2, 0)[:, None]
    row_ids = (first + jnp.arange(rows, dtype=jnp.int32))[:, None, None, None]
    col_ids = jnp.arange(size, dtype=jnp.int32)
    live = (row_ids < own_sizes) & (col_ids < own_sizes)
    psi_rows = lax.dynamic_slice_in_dim(wavefunction, first, rows, 2)
    psi_rows = psi_rows.transpose(2, 0, 1, 3).astype(F32)
    value = ours + (energy - rayleigh)[None, :, None, None] * psi_rows
    return jnp.where(live, value, 0.0), rayleigh


def solution(mesh):
    ops, blks = mesh.devices.shape
    split = Mesh(mesh.devices.reshape(ops // 2, 2, blks), OP + ("blk",))
    return jax.shard_map(
        on_device,
        mesh=split,
        in_specs=(
            P(None, "blk", None, None),
            P(OP, "blk", None, None),
            P(OP, "blk", None, None),
            P(OP),
            P(),
            P(OP, None),
            P(OP),
            P(),
        ),
        out_specs=(P(OP, None, "blk", None), P()),
        check_vma=False,
    )
```

```python
import functools

import jax
import jax.numpy as jnp
from jax import lax
from jax.experimental import pallas as pl
from jax.experimental.pallas import tpu as pltpu
from jax.sharding import Mesh, PartitionSpec as P

F32, F16, BF16 = jnp.float32, jnp.float16, jnp.bfloat16
OP = ("chip", "core")
HEAD, PIECE = 1024.0, 2048.0
TILES = 4
LANES = 128
SMEM = pl.BlockSpec(memory_space=pltpu.SMEM)
VMEM = pl.BlockSpec(memory_space=pltpu.VMEM)
HBM = pl.BlockSpec(memory_space=pltpu.HBM)
CORE, BLK, CHIP, SHIFTS = 0, 1, 2, 3


def prep_kernel(coef, energy, shifts, sizes, psi, words, edge, table, sems):
    core = lax.axis_index("core")
    copies = [
        pltpu.make_async_copy(psi.at[v, 1 - core], edge.at[v], sems.at[v]) for v in range(2)
    ]
    for copy in copies:
        copy.start()
    table[CORE] = core
    table[BLK] = lax.axis_index("blk")
    table[CHIP] = lax.axis_index("chip")
    pairs, sectors = shifts.shape[0], sizes.shape[0]
    for k in range(pairs):
        table[SHIFTS + k] = shifts[k]
    for b in range(sectors):
        table[SHIFTS + pairs + b] = sizes[b]
    spot = lax.broadcasted_iota(jnp.int32, (2, LANES), 1)
    row = lax.broadcasted_iota(jnp.int32, (2, LANES), 0)
    facts = jnp.where(spot == 0, energy[0], 0.0)
    for k in range(pairs):
        facts = jnp.where(spot == 1 + k, shifts[k].astype(F32), facts)
    lines = coef.shape[1] // LANES
    each = words.shape[0] // lines
    for i in range(lines):
        line = jnp.broadcast_to(coef[0:1, i * LANES : (i + 1) * LANES], (2, LANES))
        block = jnp.where(row == 0, line, facts)
        words[i * each : (i + 1) * each] = jnp.broadcast_to(block[None], (each, 2, LANES))
    for copy in copies:
        copy.wait()


def prepared(ops, coef, energy, shifts, sizes, psi):
    size = psi.shape[2]
    return pl.pallas_call(
        prep_kernel,
        in_specs=[VMEM] + [SMEM] * 3 + [HBM],
        out_specs=[VMEM, HBM, SMEM],
        out_shape=[
            jax.ShapeDtypeStruct((ops, 2, LANES), F32),
            jax.ShapeDtypeStruct((2, size, size), BF16),
            jax.ShapeDtypeStruct((SHIFTS + shifts.shape[0] + sizes.shape[0],), jnp.int32),
        ],
        scratch_shapes=[pltpu.SemaphoreType.DMA((2,))],
        compiler_params=pltpu.CompilerParams(vmem_limit_bytes=60_000_000),
        name="prepared",
    )(coef, energy, shifts, sizes, psi)


def loads(core, left, right, lefts, rights, sems):
    return [
        (
            pltpu.make_async_copy(left.at[k, core], lefts.at[k], sems.at[0, k]),
            pltpu.make_async_copy(right.at[k, core], rights.at[k], sems.at[1, k]),
        )
        for k in range(lefts.shape[0])
    ]


def product(core, shift, src, left, right, copies):
    size = left.shape[0]
    copies[0].wait()
    slot = core - shift
    slot = jnp.where((slot == 0) | (slot == 1), slot, 2)
    part = jnp.dot(left[...], src[slot], preferred_element_type=F32).astype(BF16)
    copies[1].wait()
    return [
        lax.dot_general(
            part[:, v * size : (v + 1) * size],
            right[...],
            (((1,), (1,)), ((), ())),
            preferred_element_type=F32,
        )
        for v in range(2)
    ]


def own_kernel(
    sectors, table, psi, halo, left, right, left_got, right_got, terms, sources,
    psis, halos, lefts, rights, made, src, sems, out_sems, more,
):
    core, blk = table[CORE], table[BLK]
    pairs, size = lefts.shape[0], lefts.shape[1]
    psi_copy = pltpu.make_async_copy(psi, psis, more.at[0])
    halo_copy = pltpu.make_async_copy(halo, halos, more.at[1])
    psi_copy.start()
    halo_copy.start()
    copies = loads(core, left, right, lefts, rights, sems)
    for pair in copies:
        for copy in pair:
            copy.start()
    row = lax.broadcasted_iota(jnp.int32, (size, size), 0)
    col = lax.broadcasted_iota(jnp.int32, (size, size), 1)
    reach = jnp.maximum(row, col)
    sizes = SHIFTS + pairs
    far = 2 * blk - 1 + 3 * core
    inside = (far >= 0) & (far < sectors)
    far_size = jnp.where(inside, table[sizes + jnp.clip(far, 0, sectors - 1)], 0)
    live_sizes = (table[sizes + 2 * blk], table[sizes + 2 * blk + 1], far_size)
    psi_copy.wait()
    halo_copy.wait()
    for slot, live_size in enumerate(live_sizes):
        live = jnp.where(reach < live_size, 1.0, 0.0).astype(BF16)
        for v in range(2):
            block = psis[v, slot] if slot < 2 else halos[v]
            src[slot, :, v * size : (v + 1) * size] = block * live
    source_copy = pltpu.make_async_copy(src, sources, more.at[2])
    source_copy.start()
    outs = []
    for k in range(pairs):
        terms_k = product(core, table[SHIFTS + k], src, lefts.at[k], rights.at[k], copies[k])
        for v in range(2):
            made[k, v] = terms_k[v]
        outs.append(pltpu.make_async_copy(made.at[k], terms.at[k], out_sems.at[k]))
        outs[k].start()
    source_copy.wait()
    for out in outs:
        out.wait()


def estimate(pairs, size):
    return pl.CostEstimate(
        flops=8 * pairs * size**3, bytes_accessed=20 * pairs * size * size, transcendentals=0
    )


def own_terms(sectors, table, psi, halo, left, right, left_got, right_got):
    pairs, _, size, _ = left.shape
    return pl.pallas_call(
        functools.partial(own_kernel, sectors),
        in_specs=[SMEM] + [HBM] * 6,
        out_specs=[HBM, HBM],
        out_shape=[
            jax.ShapeDtypeStruct((pairs, 2, size, size), F32),
            jax.ShapeDtypeStruct((3, size, 2 * size), BF16),
        ],
        scratch_shapes=[
            pltpu.VMEM(psi.shape, BF16),
            pltpu.VMEM(halo.shape, BF16),
            pltpu.VMEM((pairs, size, size), BF16),
            pltpu.VMEM((pairs, size, size), BF16),
            pltpu.VMEM((pairs, 2, size, size), F32),
            pltpu.VMEM((3, size, 2 * size), BF16),
            pltpu.SemaphoreType.DMA((2, pairs)),
            pltpu.SemaphoreType.DMA((pairs,)),
            pltpu.SemaphoreType.DMA((3,)),
        ],
        compiler_params=pltpu.CompilerParams(vmem_limit_bytes=62_850_000),
        cost_estimate=estimate(pairs, size),
        name="own_terms",
    )(table, psi, halo, left, right, left_got, right_got)


def level_of(top, head):
    return jnp.maximum(jnp.ceil(jnp.log2(jnp.maximum(top, 1e-30))), -90.0) - head


def folded(values):
    rows, columns = values.shape
    total = None
    for r in range(0, rows, 8):
        for c in range(0, columns, LANES):
            part = values[r : r + 8, c : c + LANES]
            total = part if total is None else total + part
    return total


def sigma_kernel(
    table, owner, words, own, sources, left, right, packed, norm,
    lefts, rights, owns, src, acc, sems, own_sems, more,
):
    core, chip = table[CORE], table[CHIP]
    pairs, size = lefts.shape[0], lefts.shape[1]
    source_copy = pltpu.make_async_copy(sources, src, more.at[0])
    source_copy.start()
    copies = loads(core, left, right, lefts, rights, sems)
    own_copies = [
        pltpu.make_async_copy(own.at[k], owns.at[k], own_sems.at[k]) for k in range(pairs)
    ]
    for k in range(pairs):
        copies[k][0].start()
        copies[k][1].start()
    for k in range(pairs):
        own_copies[k].start()

    chips = packed.shape[0]
    chip_rows = size // chips
    parts = size // LANES
    tag = 2 * parts * chip_rows
    tagged = packed.shape[1] - tag
    line = jnp.broadcast_to(words[owner[0], 0:1, :], (8, LANES))
    first = lax.rem(chip * 2 * pairs, LANES)
    own_weight = pltpu.roll(line, LANES - first - core * pairs, 1)
    got_weight = pltpu.roll(line, LANES - first - (1 - core) * pairs, 1)
    facts = words[2 * chip + 1 - core, 1:2, :]
    spot = lax.broadcasted_iota(jnp.int32, (1, LANES), 1)
    shifts = [
        jnp.sum(jnp.where(spot == 1 + k, facts, 0.0)).astype(jnp.int32) for k in range(pairs)
    ]

    source_copy.wait()
    for k in range(pairs):
        terms = product(core, shifts[k], src, lefts.at[k], rights.at[k], copies[k])
        for v in range(2):
            total = got_weight[0:1, k : k + 1] * terms[v]
            acc[v] = total if k == 0 else acc[v] + total
    for k in range(pairs):
        own_copies[k].wait()

    tile = size // TILES
    here = chips // TILES
    row = lax.broadcasted_iota(jnp.int32, (tagged, LANES), 0)
    lane = lax.broadcasted_iota(jnp.int32, (tagged, LANES), 1)
    sums = [None] * 4
    for step in range(TILES):
        rows = slice(step * tile, (step + 1) * tile)
        top = None
        for v in range(2):
            total = acc[v, rows, :]
            for k in range(pairs):
                total += own_weight[0:1, k : k + 1] * owns[k, v, rows, :]
            acc[v, rows, :] = total
            psi = src[core, rows, v * size : (v + 1) * size].astype(F32)
            for i, part in ((v, folded(psi * total)), (2 + v, folded(psi * psi))):
                sums[i] = part if sums[i] is None else sums[i] + part
            high = jnp.max(jnp.abs(total), keepdims=True)
            top = high if top is None else jnp.maximum(top, high)
        level = level_of(top, 14.0)
        scale = jnp.exp2(-level)
        mark = jnp.where(row == 0, level, 0.0)
        for v in range(2):
            for j in range(here):
                chip_at = step * here + j
                for t in range(parts):
                    at = (v * parts + t) * chip_rows
                    packed[chip_at, at : at + chip_rows, :] = scale * acc[
                        v, chip_at * chip_rows : (chip_at + 1) * chip_rows, t * LANES : (t + 1) * LANES
                    ]
        for j in range(here):
            packed[step * here + j, tag:, :] = mark

    cross = [jnp.sum(sums[v], keepdims=True) for v in range(2)]
    level = level_of(jnp.maximum(jnp.abs(cross[0]), jnp.abs(cross[1])), 0.0)
    values = [level]
    rest = [value * jnp.exp2(-level) * HEAD for value in cross]
    for _ in range(3):
        heads = [jnp.round(value) for value in rest]
        values += heads
        rest = [(value - head) * PIECE for value, head in zip(rest, heads)]
    tags = jnp.zeros((tagged, LANES), F32)
    for i, value in enumerate(values):
        tags = jnp.where((row == 0) & (lane == i + 1), value, tags)
    for j in range(chips):
        packed[j, tag:, :] = jnp.where(lane == 0, packed[j, tag:, :], tags)
    for v in range(2):
        norm[v : v + 1, :] = jnp.broadcast_to(jnp.sum(sums[2 + v], keepdims=True), (1, LANES))


def sigma_blocks(chips, table, owner, words, own, sources, left, right):
    pairs, _, size, _ = left.shape
    lines = -(-(2 * size * size // chips // LANES + 1) // 8) * 8
    return pl.pallas_call(
        sigma_kernel,
        in_specs=[SMEM] * 2 + [VMEM] + [HBM] * 4,
        out_specs=[VMEM, VMEM],
        out_shape=[
            jax.ShapeDtypeStruct((chips, lines, LANES), F32),
            jax.ShapeDtypeStruct((2, LANES), F32),
        ],
        scratch_shapes=[
            pltpu.VMEM((pairs, size, size), BF16),
            pltpu.VMEM((pairs, size, size), BF16),
            pltpu.VMEM((pairs, 2, size, size), F32),
            pltpu.VMEM((3, size, 2 * size), BF16),
            pltpu.VMEM((2, size, size), F32),
            pltpu.SemaphoreType.DMA((2, pairs)),
            pltpu.SemaphoreType.DMA((pairs,)),
            pltpu.SemaphoreType.DMA((1,)),
        ],
        compiler_params=pltpu.CompilerParams(vmem_limit_bytes=55_000_000),
        cost_estimate=estimate(pairs, size),
        name="sigma_blocks",
    )(table, owner, words, own, sources, left, right)


def on_device(
    wavefunction, left_ops, right_ops, shifts, sector_sizes, site_coef, site_energy, site_owner
):
    size = wavefunction.shape[2]
    pairs = left_ops.shape[0]
    chips, blks = lax.axis_size("chip"), lax.axis_size("blk")
    chip, core, blk = lax.axis_index("chip"), lax.axis_index("core"), lax.axis_index("blk")
    chip_rows = size // chips
    rows = chip_rows // 2
    parts = size // LANES
    words, edge, table = prepared(
        2 * chips, site_coef, site_energy, shifts, sector_sizes, wavefunction
    )

    swap = [(0, 1), (1, 0)]
    halo_path = [(x, x + 1) for x in range(blks - 1)] + [
        (blks + x + 1, blks + x) for x in range(blks - 1)
    ]
    halo = lax.ppermute(edge, ("core", "blk"), halo_path)
    words = lax.all_to_all(words, OP, 0, 0, tiled=True)
    left_got = lax.ppermute(left_ops, "core", swap)
    right_got = lax.ppermute(right_ops, "core", swap)
    own, sources = own_terms(
        sector_sizes.shape[0],
        table,
        wavefunction,
        halo,
        left_ops,
        right_ops,
        left_got,
        right_got,
    )
    packed, norm = sigma_blocks(
        chips, table, site_owner, words, own, sources, left_got, right_got
    )

    blocks = lax.all_to_all(packed.astype(F16), "chip", 0, 0, tiled=True)
    tag = 2 * parts * chip_rows
    tags = blocks[:, tag, :8].astype(F32)
    cross = jnp.sum(
        (tags[:, 2:4] + (tags[:, 4:6] + tags[:, 6:8] / PIECE) / PIECE)
        / HEAD
        * jnp.exp2(tags[:, 1:2]),
        axis=0,
    )
    summed = jnp.sum(blocks[:, :tag].astype(F32) * jnp.exp2(tags[:, 0])[:, None, None], axis=0)

    halves = summed.reshape(2 * parts, 2, rows, LANES).transpose(1, 0, 2, 3)
    halves = halves.reshape(2, 1, 2 * parts * rows, LANES)
    halves = jnp.broadcast_to(halves, (2, blks) + halves.shape[2:])
    sums = jnp.pad(jnp.concatenate([cross, norm[:, 0]]), (0, LANES - 4))
    sums = jnp.broadcast_to(sums[None, None, None], (2, blks, 1, LANES))
    sent = jnp.concatenate([halves, sums], axis=2).reshape(2 * blks, -1, LANES)
    came = lax.all_to_all(sent, ("core", "blk"), 0, 0, tiled=True)
    sums = jnp.sum(came[:, -1, :4], axis=0)
    energy = lax.dynamic_index_in_dim(words[:, 1, 0], site_owner[0], 0, keepdims=False)
    cross_sum, norm_sum = sums[:2], sums[2:]
    rayleigh = (cross_sum + energy * norm_sum) / (norm_sum + 1e-06)
    ours = lax.dynamic_index_in_dim(came.reshape(2, blks, -1, LANES), blk, 1, keepdims=False)
    ours = ours[:, :-1].reshape(2, 2, parts, rows, LANES).transpose(3, 1, 0, 2, 4)
    ours = ours.reshape(rows, 2, 2, size)

    first = (chip * 2 + core) * rows
    own_sizes = lax.dynamic_slice_in_dim(sector_sizes, 2 * blk, 2, 0)[:, None]
    row_ids = (first + jnp.arange(rows, dtype=jnp.int32))[:, None, None, None]
    col_ids = jnp.arange(size, dtype=jnp.int32)
    live = (row_ids < own_sizes) & (col_ids < own_sizes)
    psi_rows = lax.dynamic_slice_in_dim(wavefunction, first, rows, 2)
    psi_rows = psi_rows.transpose(2, 0, 1, 3).astype(F32)
    value = ours + (energy - rayleigh)[None, :, None, None] * psi_rows
    return jnp.where(live, value, 0.0), rayleigh


def solution(mesh):
    ops, blks = mesh.devices.shape
    split = Mesh(mesh.devices.reshape(ops // 2, 2, blks), OP + ("blk",))
    return jax.shard_map(
        on_device,
        mesh=split,
        in_specs=(
            P(None, "blk", None, None),
            P(OP, "blk", None, None),
            P(OP, "blk", None, None),
            P(OP),
            P(),
            P(OP, None),
            P(OP),
            P(),
        ),
        out_specs=(P(OP, None, "blk", None), P()),
        check_vma=False,
    )
```

```python
import functools

import jax
import jax.numpy as jnp
from jax import lax
from jax.experimental import pallas as pl
from jax.experimental.pallas import tpu as pltpu
from jax.sharding import Mesh, PartitionSpec as P

F32, F16, BF16 = jnp.float32, jnp.float16, jnp.bfloat16
OP = ("chip", "core")
HEAD, PIECE = 1024.0, 2048.0
TILES = 4
LANES = 128
SMEM = pl.BlockSpec(memory_space=pltpu.SMEM)
VMEM = pl.BlockSpec(memory_space=pltpu.VMEM)
HBM = pl.BlockSpec(memory_space=pltpu.HBM)
CORE, BLK, CHIP, SHIFTS = 0, 1, 2, 3


def prep_kernel(coef, energy, shifts, sizes, psi, words, edge, table, sems):
    core = lax.axis_index("core")
    copies = [
        pltpu.make_async_copy(psi.at[v, 1 - core], edge.at[v], sems.at[v]) for v in range(2)
    ]
    for copy in copies:
        copy.start()
    table[CORE] = core
    table[BLK] = lax.axis_index("blk")
    table[CHIP] = lax.axis_index("chip")
    pairs, sectors = shifts.shape[0], sizes.shape[0]
    for k in range(pairs):
        table[SHIFTS + k] = shifts[k]
    for b in range(sectors):
        table[SHIFTS + pairs + b] = sizes[b]
    spot = lax.broadcasted_iota(jnp.int32, (2, LANES), 1)
    row = lax.broadcasted_iota(jnp.int32, (2, LANES), 0)
    facts = jnp.where(spot == 0, energy[0], 0.0)
    for k in range(pairs):
        facts = jnp.where(spot == 1 + k, shifts[k].astype(F32), facts)
    lines = coef.shape[1] // LANES
    each = words.shape[0] // lines
    for i in range(lines):
        line = jnp.broadcast_to(coef[0:1, i * LANES : (i + 1) * LANES], (2, LANES))
        block = jnp.where(row == 0, line, facts)
        words[i * each : (i + 1) * each] = jnp.broadcast_to(block[None], (each, 2, LANES))
    for copy in copies:
        copy.wait()


def prepared(ops, coef, energy, shifts, sizes, psi):
    size = psi.shape[2]
    return pl.pallas_call(
        prep_kernel,
        in_specs=[VMEM] + [SMEM] * 3 + [HBM],
        out_specs=[VMEM, VMEM, SMEM],
        out_shape=[
            jax.ShapeDtypeStruct((ops, 2, LANES), F32),
            jax.ShapeDtypeStruct((2, size, size), BF16),
            jax.ShapeDtypeStruct((SHIFTS + shifts.shape[0] + sizes.shape[0],), jnp.int32),
        ],
        scratch_shapes=[pltpu.SemaphoreType.DMA((2,))],
        compiler_params=pltpu.CompilerParams(vmem_limit_bytes=60000000),
        name="prepared",
    )(coef, energy, shifts, sizes, psi)


def loads(core, left, right, lefts, rights, sems):
    return [
        (
            pltpu.make_async_copy(left.at[k, core], lefts.at[k], sems.at[0, k]),
            pltpu.make_async_copy(right.at[k, core], rights.at[k], sems.at[1, k]),
        )
        for k in range(lefts.shape[0])
    ]


def product(core, shift, src, left, right, copies):
    size = left.shape[0]
    copies[0].wait()
    slot = core - shift
    slot = jnp.where((slot == 0) | (slot == 1), slot, 2)
    part = jnp.dot(left[...], src[slot], preferred_element_type=F32).astype(BF16)
    copies[1].wait()
    return [
        lax.dot_general(
            part[:, v * size : (v + 1) * size],
            right[...],
            (((1,), (1,)), ((), ())),
            preferred_element_type=F32,
        )
        for v in range(2)
    ]


def own_kernel(
    sectors, table, psi, halo, left, right, terms, sources,
    psis, halos, lefts, rights, made, src, sems, out_sems, more,
):
    core, blk = table[CORE], table[BLK]
    pairs, size = lefts.shape[0], lefts.shape[1]
    psi_copy = pltpu.make_async_copy(psi, psis, more.at[0])
    halo_copy = pltpu.make_async_copy(halo, halos, more.at[1])
    psi_copy.start()
    halo_copy.start()
    copies = loads(core, left, right, lefts, rights, sems)
    for pair in copies:
        for copy in pair:
            copy.start()
    row = lax.broadcasted_iota(jnp.int32, (size, size), 0)
    col = lax.broadcasted_iota(jnp.int32, (size, size), 1)
    reach = jnp.maximum(row, col)
    sizes = SHIFTS + pairs
    far = 2 * blk - 1 + 3 * core
    inside = (far >= 0) & (far < sectors)
    far_size = jnp.where(inside, table[sizes + jnp.clip(far, 0, sectors - 1)], 0)
    live_sizes = (table[sizes + 2 * blk], table[sizes + 2 * blk + 1], far_size)
    psi_copy.wait()
    halo_copy.wait()
    for slot, live_size in enumerate(live_sizes):
        live = jnp.where(reach < live_size, 1.0, 0.0).astype(BF16)
        for v in range(2):
            block = psis[v, slot] if slot < 2 else halos[v]
            src[slot, :, v * size : (v + 1) * size] = block * live
    source_copy = pltpu.make_async_copy(src, sources, more.at[2])
    outs = []
    for k in range(pairs):
        terms_k = product(core, table[SHIFTS + k], src, lefts.at[k], rights.at[k], copies[k])
        for v in range(2):
            made[k, v] = terms_k[v]
            outs.append(
                pltpu.make_async_copy(made.at[k, v], terms.at[k, v], out_sems.at[2 * k + v])
            )
            outs[-1].start()
        if k == 0:
            source_copy.start()
    source_copy.wait()
    for out in outs:
        out.wait()


def estimate(pairs, size):
    return pl.CostEstimate(
        flops=8 * pairs * size**3, bytes_accessed=20 * pairs * size * size, transcendentals=0
    )


def own_terms(sectors, table, psi, halo, left, right):
    pairs, _, size, _ = left.shape
    return pl.pallas_call(
        functools.partial(own_kernel, sectors),
        in_specs=[SMEM] + [HBM] * 4,
        out_specs=[HBM, HBM],
        out_shape=[
            jax.ShapeDtypeStruct((pairs, 2, size, size), F32),
            jax.ShapeDtypeStruct((3, size, 2 * size), BF16),
        ],
        scratch_shapes=[
            pltpu.VMEM(psi.shape, BF16),
            pltpu.VMEM(halo.shape, BF16),
            pltpu.VMEM((pairs, size, size), BF16),
            pltpu.VMEM((pairs, size, size), BF16),
            pltpu.VMEM((pairs, 2, size, size), F32),
            pltpu.VMEM((3, size, 2 * size), BF16),
            pltpu.SemaphoreType.DMA((2, pairs)),
            pltpu.SemaphoreType.DMA((2 * pairs,)),
            pltpu.SemaphoreType.DMA((3,)),
        ],
        compiler_params=pltpu.CompilerParams(vmem_limit_bytes=56200000),
        cost_estimate=estimate(100 * pairs, size),
        name="own_terms",
    )(table, psi, halo, left, right)


def level_of(top, head):
    return jnp.maximum(jnp.ceil(jnp.log2(jnp.maximum(top, 1e-30))), -90.0) - head


def folded(values):
    rows, columns = values.shape
    total = None
    for r in range(0, rows, 8):
        for c in range(0, columns, LANES):
            part = values[r : r + 8, c : c + LANES]
            total = part if total is None else total + part
    return total


def sigma_kernel(
    table, owner, words, own, sources, left, right, packed, norm,
    lefts, rights, owns, src, acc, sems, own_sems, more,
):
    core, chip = table[CORE], table[CHIP]
    pairs, size = lefts.shape[0], lefts.shape[1]
    source_copy = pltpu.make_async_copy(sources, src, more.at[0])
    source_copy.start()
    copies = loads(core, left, right, lefts, rights, sems)
    own_copies = [
        pltpu.make_async_copy(own.at[k], owns.at[k], own_sems.at[k]) for k in range(pairs)
    ]
    for k in range(pairs):
        copies[k][0].start()
        copies[k][1].start()
    for k in range(pairs):
        own_copies[k].start()

    chips = packed.shape[0]
    chip_rows = size // chips
    parts = size // LANES
    tag = 2 * parts * chip_rows
    tagged = packed.shape[1] - tag
    line = jnp.broadcast_to(words[owner[0], 0:1, :], (8, LANES))
    first = lax.rem(chip * 2 * pairs, LANES)
    own_weight = pltpu.roll(line, LANES - first - core * pairs, 1)
    got_weight = pltpu.roll(line, LANES - first - (1 - core) * pairs, 1)
    facts = words[2 * chip + 1 - core, 1:2, :]
    spot = lax.broadcasted_iota(jnp.int32, (1, LANES), 1)
    shifts = [
        jnp.sum(jnp.where(spot == 1 + k, facts, 0.0)).astype(jnp.int32) for k in range(pairs)
    ]

    source_copy.wait()
    for k in range(pairs):
        terms = product(core, shifts[k], src, lefts.at[k], rights.at[k], copies[k])
        for v in range(2):
            total = got_weight[0:1, k : k + 1] * terms[v]
            acc[v] = total if k == 0 else acc[v] + total
    for k in range(pairs):
        own_copies[k].wait()

    tile = size // TILES
    here = chips // TILES
    row = lax.broadcasted_iota(jnp.int32, (tagged, LANES), 0)
    lane = lax.broadcasted_iota(jnp.int32, (tagged, LANES), 1)
    sums = [None] * 4
    for step in range(TILES):
        rows = slice(step * tile, (step + 1) * tile)
        top = None
        for v in range(2):
            total = acc[v, rows, :]
            for k in range(pairs):
                total += own_weight[0:1, k : k + 1] * owns[k, v, rows, :]
            acc[v, rows, :] = total
            psi = src[core, rows, v * size : (v + 1) * size].astype(F32)
            for i, part in ((v, folded(psi * total)), (2 + v, folded(psi * psi))):
                sums[i] = part if sums[i] is None else sums[i] + part
            high = jnp.max(jnp.abs(total), keepdims=True)
            top = high if top is None else jnp.maximum(top, high)
        level = level_of(top, 14.0)
        scale = jnp.exp2(-level)
        mark = jnp.where(row == 0, level, 0.0)
        for v in range(2):
            for j in range(here):
                chip_at = step * here + j
                for t in range(parts):
                    at = (v * parts + t) * chip_rows
                    packed[chip_at, at : at + chip_rows, :] = scale * acc[
                        v, chip_at * chip_rows : (chip_at + 1) * chip_rows, t * LANES : (t + 1) * LANES
                    ]
        for j in range(here):
            packed[step * here + j, tag:, :] = mark

    cross = [jnp.sum(sums[v], keepdims=True) for v in range(2)]
    level = level_of(jnp.maximum(jnp.abs(cross[0]), jnp.abs(cross[1])), 0.0)
    values = [level]
    rest = [value * jnp.exp2(-level) * HEAD for value in cross]
    for _ in range(3):
        heads = [jnp.round(value) for value in rest]
        values += heads
        rest = [(value - head) * PIECE for value, head in zip(rest, heads)]
    tags = jnp.zeros((tagged, LANES), F32)
    for i, value in enumerate(values):
        tags = jnp.where((row == 0) & (lane == i + 1), value, tags)
    for j in range(chips):
        packed[j, tag:, :] = jnp.where(lane == 0, packed[j, tag:, :], tags)
    for v in range(2):
        norm[v : v + 1, :] = jnp.broadcast_to(jnp.sum(sums[2 + v], keepdims=True), (1, LANES))


def sigma_blocks(chips, table, owner, words, own, sources, left, right):
    pairs, _, size, _ = left.shape
    lines = -(-(2 * size * size // chips // LANES + 1) // 8) * 8
    return pl.pallas_call(
        sigma_kernel,
        in_specs=[SMEM] * 2 + [VMEM] + [HBM] * 4,
        out_specs=[VMEM, VMEM],
        out_shape=[
            jax.ShapeDtypeStruct((chips, lines, LANES), F32),
            jax.ShapeDtypeStruct((2, LANES), F32),
        ],
        scratch_shapes=[
            pltpu.VMEM((pairs, size, size), BF16),
            pltpu.VMEM((pairs, size, size), BF16),
            pltpu.VMEM((pairs, 2, size, size), F32),
            pltpu.VMEM((3, size, 2 * size), BF16),
            pltpu.VMEM((2, size, size), F32),
            pltpu.SemaphoreType.DMA((2, pairs)),
            pltpu.SemaphoreType.DMA((pairs,)),
            pltpu.SemaphoreType.DMA((1,)),
        ],
        compiler_params=pltpu.CompilerParams(vmem_limit_bytes=55_000_000),
        cost_estimate=estimate(pairs, size),
        name="sigma_blocks",
    )(table, owner, words, own, sources, left, right)


def on_device(
    wavefunction, left_ops, right_ops, shifts, sector_sizes, site_coef, site_energy, site_owner
):
    size = wavefunction.shape[2]
    pairs = left_ops.shape[0]
    chips, blks = lax.axis_size("chip"), lax.axis_size("blk")
    chip, core, blk = lax.axis_index("chip"), lax.axis_index("core"), lax.axis_index("blk")
    chip_rows = size // chips
    rows = chip_rows // 2
    parts = size // LANES
    words, edge, table = prepared(
        2 * chips, site_coef, site_energy, shifts, sector_sizes, wavefunction
    )

    swap = [(0, 1), (1, 0)]
    halo_path = [(x, x + 1) for x in range(blks - 1)] + [
        (blks + x + 1, blks + x) for x in range(blks - 1)
    ]
    halo = lax.ppermute(edge, ("core", "blk"), halo_path)
    words = lax.all_to_all(words, OP, 0, 0, tiled=True)
    left_got = lax.ppermute(left_ops, "core", swap)
    right_got = lax.ppermute(right_ops, "core", swap)
    own, sources = own_terms(
        sector_sizes.shape[0],
        table,
        wavefunction,
        halo,
        left_ops,
        right_ops,
    )
    packed, norm = sigma_blocks(
        chips, table, site_owner, words, own, sources, left_got, right_got
    )

    blocks = lax.all_to_all(packed.astype(F16), "chip", 0, 0, tiled=True)
    tag = 2 * parts * chip_rows
    tags = blocks[:, tag, :8].astype(F32)
    cross = jnp.sum(
        (tags[:, 2:4] + (tags[:, 4:6] + tags[:, 6:8] / PIECE) / PIECE)
        / HEAD
        * jnp.exp2(tags[:, 1:2]),
        axis=0,
    )
    summed = jnp.sum(blocks[:, :tag].astype(F32) * jnp.exp2(tags[:, 0])[:, None, None], axis=0)

    halves = summed.reshape(2 * parts, 2, rows, LANES).transpose(1, 0, 2, 3)
    halves = halves.reshape(2, 1, 2 * parts * rows, LANES)
    halves = jnp.broadcast_to(halves, (2, blks) + halves.shape[2:])
    sums = jnp.pad(jnp.concatenate([cross, norm[:, 0]]), (0, LANES - 4))
    sums = jnp.broadcast_to(sums[None, None, None], (2, blks, 1, LANES))
    sent = jnp.concatenate([halves, sums], axis=2).reshape(2 * blks, -1, LANES)
    came = lax.all_to_all(sent, ("core", "blk"), 0, 0, tiled=True)
    sums = jnp.sum(came[:, -1, :4], axis=0)
    energy = lax.dynamic_index_in_dim(words[:, 1, 0], site_owner[0], 0, keepdims=False)
    cross_sum, norm_sum = sums[:2], sums[2:]
    rayleigh = (cross_sum + energy * norm_sum) / (norm_sum + 1e-06)
    ours = lax.dynamic_index_in_dim(came.reshape(2, blks, -1, LANES), blk, 1, keepdims=False)
    ours = ours[:, :-1].reshape(2, 2, parts, rows, LANES).transpose(3, 1, 0, 2, 4)
    ours = ours.reshape(rows, 2, 2, size)

    first = (chip * 2 + core) * rows
    own_sizes = lax.dynamic_slice_in_dim(sector_sizes, 2 * blk, 2, 0)[:, None]
    row_ids = (first + jnp.arange(rows, dtype=jnp.int32))[:, None, None, None]
    col_ids = jnp.arange(size, dtype=jnp.int32)
    live = (row_ids < own_sizes) & (col_ids < own_sizes)
    psi_rows = lax.dynamic_slice_in_dim(wavefunction, first, rows, 2)
    psi_rows = psi_rows.transpose(2, 0, 1, 3).astype(F32)
    value = ours + (energy - rayleigh)[None, :, None, None] * psi_rows
    return jnp.where(live, value, 0.0), rayleigh


def solution(mesh):
    ops, blks = mesh.devices.shape
    split = Mesh(mesh.devices.reshape(ops // 2, 2, blks), OP + ("blk",))
    return jax.shard_map(
        on_device,
        mesh=split,
        in_specs=(
            P(None, "blk", None, None),
            P(OP, "blk", None, None),
            P(OP, "blk", None, None),
            P(OP),
            P(),
            P(OP, None),
            P(OP),
            P(),
        ),
        out_specs=(P(OP, None, "blk", None), P()),
        check_vma=False,
    )
```

```python
import functools

import jax
import jax.numpy as jnp
from jax import lax
from jax.experimental import pallas as pl
from jax.experimental.pallas import tpu as pltpu
from jax.sharding import Mesh, PartitionSpec as P

F32, F16, BF16 = jnp.float32, jnp.float16, jnp.bfloat16
OP = ("chip", "core")
HEAD, PIECE = 1024.0, 2048.0
TILES = 4
EARLY = 2
LANES = 128
SMEM = pl.BlockSpec(memory_space=pltpu.SMEM)
VMEM = pl.BlockSpec(memory_space=pltpu.VMEM)
HBM = pl.BlockSpec(memory_space=pltpu.HBM)
CORE, BLK, CHIP, SHIFTS = 0, 1, 2, 3


def prep_kernel(coef, energy, shifts, sizes, psi, words, edge, table, sems):
    core = lax.axis_index("core")
    copies = [
        pltpu.make_async_copy(psi.at[v, 1 - core], edge.at[v], sems.at[v]) for v in range(2)
    ]
    for copy in copies:
        copy.start()
    table[CORE] = core
    table[BLK] = lax.axis_index("blk")
    table[CHIP] = lax.axis_index("chip")
    pairs, sectors = shifts.shape[0], sizes.shape[0]
    for k in range(pairs):
        table[SHIFTS + k] = shifts[k]
    for b in range(sectors):
        table[SHIFTS + pairs + b] = sizes[b]
    spot = lax.broadcasted_iota(jnp.int32, (2, LANES), 1)
    row = lax.broadcasted_iota(jnp.int32, (2, LANES), 0)
    facts = jnp.where(spot == 0, energy[0], 0.0)
    for k in range(pairs):
        facts = jnp.where(spot == 1 + k, shifts[k].astype(F32), facts)
    lines = coef.shape[1] // LANES
    each = words.shape[0] // lines
    for i in range(lines):
        line = jnp.broadcast_to(coef[0:1, i * LANES : (i + 1) * LANES], (2, LANES))
        block = jnp.where(row == 0, line, facts)
        words[i * each : (i + 1) * each] = jnp.broadcast_to(block[None], (each, 2, LANES))
    for copy in copies:
        copy.wait()


def prepared(ops, coef, energy, shifts, sizes, psi):
    size = psi.shape[2]
    return pl.pallas_call(
        prep_kernel,
        in_specs=[VMEM] + [SMEM] * 3 + [HBM],
        out_specs=[VMEM, VMEM, SMEM],
        out_shape=[
            jax.ShapeDtypeStruct((ops, 2, LANES), F32),
            jax.ShapeDtypeStruct((2, size, size), BF16),
            jax.ShapeDtypeStruct((SHIFTS + shifts.shape[0] + sizes.shape[0],), jnp.int32),
        ],
        scratch_shapes=[pltpu.SemaphoreType.DMA((2,))],
        compiler_params=pltpu.CompilerParams(vmem_limit_bytes=60_000_000),
        name="prepared",
    )(coef, energy, shifts, sizes, psi)


def loads(core, left, right, lefts, rights, sems, pairs, at=0):
    return [
        (
            pltpu.make_async_copy(left.at[k, core], lefts.at[at + i], sems.at[0, at + i]),
            pltpu.make_async_copy(right.at[k, core], rights.at[at + i], sems.at[1, at + i]),
        )
        for i, k in enumerate(pairs)
    ]


def product(core, shift, src, left, right, copies):
    size = left.shape[0]
    copies[0].wait()
    slot = core - shift
    slot = jnp.where((slot == 0) | (slot == 1), slot, 2)
    part = jnp.dot(left[...], src[slot], preferred_element_type=F32).astype(BF16)
    copies[1].wait()
    return [
        lax.dot_general(
            part[:, v * size : (v + 1) * size],
            right[...],
            (((1,), (1,)), ((), ())),
            preferred_element_type=F32,
        )
        for v in range(2)
    ]


def own_kernel(
    sectors, table, psi, halo, left, right, terms, sources,
    psis, halos, lefts, rights, made, src, sems, out_sems, more,
):
    core, blk = table[CORE], table[BLK]
    early, size = lefts.shape[0], lefts.shape[1]
    pairs = left.shape[0]
    psi_copy = pltpu.make_async_copy(psi, psis, more.at[0])
    halo_copy = pltpu.make_async_copy(halo, halos, more.at[1])
    psi_copy.start()
    halo_copy.start()
    copies = loads(core, left, right, lefts, rights, sems, range(early))
    for pair in copies:
        for copy in pair:
            copy.start()
    row = lax.broadcasted_iota(jnp.int32, (size, size), 0)
    col = lax.broadcasted_iota(jnp.int32, (size, size), 1)
    reach = jnp.maximum(row, col)
    sizes = SHIFTS + pairs
    far = 2 * blk - 1 + 3 * core
    inside = (far >= 0) & (far < sectors)
    far_size = jnp.where(inside, table[sizes + jnp.clip(far, 0, sectors - 1)], 0)
    live_sizes = (table[sizes + 2 * blk], table[sizes + 2 * blk + 1], far_size)
    psi_copy.wait()
    halo_copy.wait()
    for slot, live_size in enumerate(live_sizes):
        live = jnp.where(reach < live_size, 1.0, 0.0).astype(BF16)
        for v in range(2):
            block = psis[v, slot] if slot < 2 else halos[v]
            src[slot, :, v * size : (v + 1) * size] = block * live
    source_copy = pltpu.make_async_copy(src, sources, more.at[2])
    outs = []
    for k in range(early):
        terms_k = product(core, table[SHIFTS + k], src, lefts.at[k], rights.at[k], copies[k])
        for v in range(2):
            made[k, v] = terms_k[v]
            outs.append(
                pltpu.make_async_copy(made.at[k, v], terms.at[k, v], out_sems.at[2 * k + v])
            )
            outs[-1].start()
        if k == 0:
            source_copy.start()
    source_copy.wait()
    for out in outs:
        out.wait()


def estimate(pairs, size):
    return pl.CostEstimate(
        flops=8 * pairs * size**3, bytes_accessed=20 * pairs * size * size, transcendentals=0
    )


def own_terms(sectors, table, psi, halo, left, right):
    pairs, _, size, _ = left.shape
    return pl.pallas_call(
        functools.partial(own_kernel, sectors),
        in_specs=[SMEM] + [HBM] * 4,
        out_specs=[HBM, HBM],
        out_shape=[
            jax.ShapeDtypeStruct((EARLY, 2, size, size), F32),
            jax.ShapeDtypeStruct((3, size, 2 * size), BF16),
        ],
        scratch_shapes=[
            pltpu.VMEM(psi.shape, BF16),
            pltpu.VMEM(halo.shape, BF16),
            pltpu.VMEM((EARLY, size, size), BF16),
            pltpu.VMEM((EARLY, size, size), BF16),
            pltpu.VMEM((EARLY, 2, size, size), F32),
            pltpu.VMEM((3, size, 2 * size), BF16),
            pltpu.SemaphoreType.DMA((2, EARLY)),
            pltpu.SemaphoreType.DMA((2 * EARLY,)),
            pltpu.SemaphoreType.DMA((3,)),
        ],
        compiler_params=pltpu.CompilerParams(vmem_limit_bytes=62_850_000),
        cost_estimate=estimate(100 * pairs, size),
        name="own_terms",
    )(table, psi, halo, left, right)


def level_of(top, head):
    return jnp.maximum(jnp.ceil(jnp.log2(jnp.maximum(top, 1e-30))), -90.0) - head


def folded(values):
    rows, columns = values.shape
    total = None
    for r in range(0, rows, 8):
        for c in range(0, columns, LANES):
            part = values[r : r + 8, c : c + LANES]
            total = part if total is None else total + part
    return total


def sigma_kernel(
    table, owner, words, own, sources, left, right, left_got, right_got, packed, norm,
    lefts, rights, owns, src, acc, sems, own_sems, more,
):
    core, chip = table[CORE], table[CHIP]
    pairs, size = left.shape[0], left.shape[2]
    early = own.shape[0]
    late = range(early, pairs)
    source_copy = pltpu.make_async_copy(sources, src, more.at[0])
    source_copy.start()
    copies = loads(core, left, right, lefts, rights, sems, late)
    copies += loads(core, left_got, right_got, lefts, rights, sems, range(pairs), len(late))
    own_copies = [
        pltpu.make_async_copy(own.at[k], owns.at[k], own_sems.at[k]) for k in range(early)
    ]
    for copy in [copy for pair in copies for copy in pair] + own_copies:
        copy.start()

    chips = packed.shape[0]
    chip_rows = size // chips
    parts = size // LANES
    tag = 2 * parts * chip_rows
    tagged = packed.shape[1] - tag
    line = jnp.broadcast_to(words[owner[0], 0:1, :], (8, LANES))
    first = lax.rem(chip * 2 * pairs, LANES)
    own_weight = pltpu.roll(line, LANES - first - core * pairs, 1)
    got_weight = pltpu.roll(line, LANES - first - (1 - core) * pairs, 1)
    facts = words[2 * chip + 1 - core, 1:2, :]
    spot = lax.broadcasted_iota(jnp.int32, (1, LANES), 1)
    shifts = [table[SHIFTS + k] for k in late]
    shifts += [
        jnp.sum(jnp.where(spot == 1 + k, facts, 0.0)).astype(jnp.int32) for k in range(pairs)
    ]

    source_copy.wait()
    weights = [own_weight[0:1, k : k + 1] for k in late]
    weights += [got_weight[0:1, k : k + 1] for k in range(pairs)]
    for i, weight in enumerate(weights):
        terms = product(core, shifts[i], src, lefts.at[i], rights.at[i], copies[i])
        for v in range(2):
            total = weight * terms[v]
            acc[v] = total if i == 0 else acc[v] + total
    for copy in own_copies:
        copy.wait()

    tile = size // TILES
    here = chips // TILES
    row = lax.broadcasted_iota(jnp.int32, (tagged, LANES), 0)
    lane = lax.broadcasted_iota(jnp.int32, (tagged, LANES), 1)
    sums = [None] * 4
    for step in range(TILES):
        rows = slice(step * tile, (step + 1) * tile)
        top = None
        for v in range(2):
            total = acc[v, rows, :]
            for k in range(early):
                total += own_weight[0:1, k : k + 1] * owns[k, v, rows, :]
            acc[v, rows, :] = total
            psi = src[core, rows, v * size : (v + 1) * size].astype(F32)
            for i, part in ((v, folded(psi * total)), (2 + v, folded(psi * psi))):
                sums[i] = part if sums[i] is None else sums[i] + part
            high = jnp.max(jnp.abs(total), keepdims=True)
            top = high if top is None else jnp.maximum(top, high)
        level = level_of(top, 14.0)
        scale = jnp.exp2(-level)
        mark = jnp.where(row == 0, level, 0.0)
        for v in range(2):
            for j in range(here):
                chip_at = step * here + j
                for t in range(parts):
                    at = (v * parts + t) * chip_rows
                    packed[chip_at, at : at + chip_rows, :] = scale * acc[
                        v, chip_at * chip_rows : (chip_at + 1) * chip_rows, t * LANES : (t + 1) * LANES
                    ]
        for j in range(here):
            packed[step * here + j, tag:, :] = mark

    cross = [jnp.sum(sums[v], keepdims=True) for v in range(2)]
    level = level_of(jnp.maximum(jnp.abs(cross[0]), jnp.abs(cross[1])), 0.0)
    values = [level]
    rest = [value * jnp.exp2(-level) * HEAD for value in cross]
    for _ in range(3):
        heads = [jnp.round(value) for value in rest]
        values += heads
        rest = [(value - head) * PIECE for value, head in zip(rest, heads)]
    tags = jnp.zeros((tagged, LANES), F32)
    for i, value in enumerate(values):
        tags = jnp.where((row == 0) & (lane == i + 1), value, tags)
    for j in range(chips):
        packed[j, tag:, :] = jnp.where(lane == 0, packed[j, tag:, :], tags)
    for v in range(2):
        norm[v : v + 1, :] = jnp.broadcast_to(jnp.sum(sums[2 + v], keepdims=True), (1, LANES))


def sigma_blocks(chips, table, owner, words, own, sources, left, right, left_got, right_got):
    pairs, _, size, _ = left.shape
    lines = -(-(2 * size * size // chips // LANES + 1) // 8) * 8
    return pl.pallas_call(
        sigma_kernel,
        in_specs=[SMEM] * 2 + [VMEM] + [HBM] * 6,
        out_specs=[VMEM, VMEM],
        out_shape=[
            jax.ShapeDtypeStruct((chips, lines, LANES), F32),
            jax.ShapeDtypeStruct((2, LANES), F32),
        ],
        scratch_shapes=[
            pltpu.VMEM((2 * pairs - EARLY, size, size), BF16),
            pltpu.VMEM((2 * pairs - EARLY, size, size), BF16),
            pltpu.VMEM((EARLY, 2, size, size), F32),
            pltpu.VMEM((3, size, 2 * size), BF16),
            pltpu.VMEM((2, size, size), F32),
            pltpu.SemaphoreType.DMA((2, 2 * pairs - EARLY)),
            pltpu.SemaphoreType.DMA((EARLY,)),
            pltpu.SemaphoreType.DMA((1,)),
        ],
        compiler_params=pltpu.CompilerParams(vmem_limit_bytes=55_000_000),
        cost_estimate=estimate(pairs, size),
        name="sigma_blocks",
    )(table, owner, words, own, sources, left, right, left_got, right_got)


def on_device(
    wavefunction, left_ops, right_ops, shifts, sector_sizes, site_coef, site_energy, site_owner
):
    size = wavefunction.shape[2]
    pairs = left_ops.shape[0]
    chips, blks = lax.axis_size("chip"), lax.axis_size("blk")
    chip, core, blk = lax.axis_index("chip"), lax.axis_index("core"), lax.axis_index("blk")
    chip_rows = size // chips
    rows = chip_rows // 2
    parts = size // LANES
    words, edge, table = prepared(
        2 * chips, site_coef, site_energy, shifts, sector_sizes, wavefunction
    )

    swap = [(0, 1), (1, 0)]
    halo_path = [(x, x + 1) for x in range(blks - 1)] + [
        (blks + x + 1, blks + x) for x in range(blks - 1)
    ]
    halo = lax.ppermute(edge, ("core", "blk"), halo_path)
    words = lax.all_to_all(words, OP, 0, 0, tiled=True)
    left_got = lax.ppermute(left_ops, "core", swap)
    right_got = lax.ppermute(right_ops, "core", swap)
    own, sources = own_terms(
        sector_sizes.shape[0],
        table,
        wavefunction,
        halo,
        left_ops,
        right_ops,
    )
    packed, norm = sigma_blocks(
        chips,
        table,
        site_owner,
        words,
        own,
        sources,
        left_ops,
        right_ops,
        left_got,
        right_got,
    )

    blocks = lax.all_to_all(packed.astype(F16), "chip", 0, 0, tiled=True)
    tag = 2 * parts * chip_rows
    tags = blocks[:, tag, :8].astype(F32)
    cross = jnp.sum(
        (tags[:, 2:4] + (tags[:, 4:6] + tags[:, 6:8] / PIECE) / PIECE)
        / HEAD
        * jnp.exp2(tags[:, 1:2]),
        axis=0,
    )
    summed = jnp.sum(blocks[:, :tag].astype(F32) * jnp.exp2(tags[:, 0])[:, None, None], axis=0)

    halves = summed.reshape(2 * parts, 2, rows, LANES).transpose(1, 0, 2, 3)
    halves = halves.reshape(2, 1, 2 * parts * rows, LANES)
    halves = jnp.broadcast_to(halves, (2, blks) + halves.shape[2:])
    sums = jnp.pad(jnp.concatenate([cross, norm[:, 0]]), (0, LANES - 4))
    sums = jnp.broadcast_to(sums[None, None, None], (2, blks, 1, LANES))
    sent = jnp.concatenate([halves, sums], axis=2).reshape(2 * blks, -1, LANES)
    came = lax.all_to_all(sent, ("core", "blk"), 0, 0, tiled=True)
    sums = jnp.sum(came[:, -1, :4], axis=0)
    energy = lax.dynamic_index_in_dim(words[:, 1, 0], site_owner[0], 0, keepdims=False)
    cross_sum, norm_sum = sums[:2], sums[2:]
    rayleigh = (cross_sum + energy * norm_sum) / (norm_sum + 1e-06)
    ours = lax.dynamic_index_in_dim(came.reshape(2, blks, -1, LANES), blk, 1, keepdims=False)
    ours = ours[:, :-1].reshape(2, 2, parts, rows, LANES).transpose(3, 1, 0, 2, 4)
    ours = ours.reshape(rows, 2, 2, size)

    first = (chip * 2 + core) * rows
    own_sizes = lax.dynamic_slice_in_dim(sector_sizes, 2 * blk, 2, 0)[:, None]
    row_ids = (first + jnp.arange(rows, dtype=jnp.int32))[:, None, None, None]
    col_ids = jnp.arange(size, dtype=jnp.int32)
    live = (row_ids < own_sizes) & (col_ids < own_sizes)
    psi_rows = lax.dynamic_slice_in_dim(wavefunction, first, rows, 2)
    psi_rows = psi_rows.transpose(2, 0, 1, 3).astype(F32)
    value = ours + (energy - rayleigh)[None, :, None, None] * psi_rows
    return jnp.where(live, value, 0.0), rayleigh


def solution(mesh):
    ops, blks = mesh.devices.shape
    split = Mesh(mesh.devices.reshape(ops // 2, 2, blks), OP + ("blk",))
    return jax.shard_map(
        on_device,
        mesh=split,
        in_specs=(
            P(None, "blk", None, None),
            P(OP, "blk", None, None),
            P(OP, "blk", None, None),
            P(OP),
            P(),
            P(OP, None),
            P(OP),
            P(),
        ),
        out_specs=(P(OP, None, "blk", None), P()),
        check_vma=False,
    )
```

```python
import functools

import jax
import jax.numpy as jnp
from jax import lax
from jax.experimental import pallas as pl
from jax.experimental.pallas import tpu as pltpu
from jax.sharding import Mesh, PartitionSpec as P

F32, F16, BF16 = jnp.float32, jnp.float16, jnp.bfloat16
OP = ("chip", "core")
HEAD, PIECE = 1024.0, 2048.0
TILES = 4
EARLY = 2
LANES = 128
SMEM = pl.BlockSpec(memory_space=pltpu.SMEM)
VMEM = pl.BlockSpec(memory_space=pltpu.VMEM)
HBM = pl.BlockSpec(memory_space=pltpu.HBM)
CORE, BLK, CHIP, SHIFTS = 0, 1, 2, 3


def prep_kernel(coef, energy, shifts, sizes, psi, words, edge, table, sems):
    core = lax.axis_index("core")
    copies = [
        pltpu.make_async_copy(psi.at[v, 1 - core], edge.at[v], sems.at[v]) for v in range(2)
    ]
    for copy in copies:
        copy.start()
    table[CORE] = core
    table[BLK] = lax.axis_index("blk")
    table[CHIP] = lax.axis_index("chip")
    pairs, sectors = shifts.shape[0], sizes.shape[0]
    for k in range(pairs):
        table[SHIFTS + k] = shifts[k]
    for b in range(sectors):
        table[SHIFTS + pairs + b] = sizes[b]
    spot = lax.broadcasted_iota(jnp.int32, (2, LANES), 1)
    row = lax.broadcasted_iota(jnp.int32, (2, LANES), 0)
    facts = jnp.where(spot == 0, energy[0:1, 0:1], 0.0)
    for k in range(pairs):
        facts = jnp.where(spot == 1 + k, shifts[k].astype(F32), facts)
    lines = coef.shape[1] // LANES
    each = words.shape[0] // lines
    for i in range(lines):
        line = jnp.broadcast_to(coef[0:1, i * LANES : (i + 1) * LANES], (2, LANES))
        block = jnp.where(row == 0, line, facts)
        words[i * each : (i + 1) * each] = jnp.broadcast_to(block[None], (each, 2, LANES))
    for copy in copies:
        copy.wait()


def prepared(ops, coef, energy, shifts, sizes, psi):
    size = psi.shape[2]
    return pl.pallas_call(
        prep_kernel,
        in_specs=[VMEM] * 2 + [SMEM] * 2 + [HBM],
        out_specs=[VMEM, VMEM, SMEM],
        out_shape=[
            jax.ShapeDtypeStruct((ops, 2, LANES), F32),
            jax.ShapeDtypeStruct((2, size, size), BF16),
            jax.ShapeDtypeStruct((SHIFTS + shifts.shape[0] + sizes.shape[0],), jnp.int32),
        ],
        scratch_shapes=[pltpu.SemaphoreType.DMA((2,))],
        compiler_params=pltpu.CompilerParams(vmem_limit_bytes=60_000_000),
        name="prepared",
    )(coef, energy, shifts, sizes, psi)


def loads(core, left, right, lefts, rights, sems, pairs, at=0):
    return [
        (
            pltpu.make_async_copy(left.at[k, core], lefts.at[at + i], sems.at[0, at + i]),
            pltpu.make_async_copy(right.at[k, core], rights.at[at + i], sems.at[1, at + i]),
        )
        for i, k in enumerate(pairs)
    ]


def slot_of(core, shift):
    slot = core - shift
    return jnp.where((slot == 0) | (slot == 1), slot, 2)


def product(slot, src, left, right):
    size = left.shape[0]
    part = jnp.dot(left[...], src[slot], preferred_element_type=F32).astype(BF16)
    part = jnp.concatenate([part[:, :size], part[:, size:]], axis=0)
    terms = lax.dot_general(
        part, right[...], (((1,), (1,)), ((), ())), preferred_element_type=F32
    )
    return [terms[:size], terms[size:]]


def wait_for(pairs):
    for copies in pairs:
        for copy in copies:
            copy.wait()


def own_kernel(
    sectors, table, psi, halo, left, right, terms, sources,
    psis, halos, lefts, rights, made, src, sems, out_sems, more,
):
    core, blk = table[CORE], table[BLK]
    early, size = lefts.shape[0], lefts.shape[1]
    pairs = left.shape[0]
    psi_copy = pltpu.make_async_copy(psi, psis, more.at[0])
    halo_copy = pltpu.make_async_copy(halo, halos, more.at[1])
    psi_copy.start()
    halo_copy.start()
    copies = loads(core, left, right, lefts, rights, sems, range(early))
    for pair in copies:
        for copy in pair:
            copy.start()
    row = lax.broadcasted_iota(jnp.int32, (size, size), 0)
    col = lax.broadcasted_iota(jnp.int32, (size, size), 1)
    reach = jnp.maximum(row, col)
    sizes = SHIFTS + pairs
    far = 2 * blk - 1 + 3 * core
    inside = (far >= 0) & (far < sectors)
    far_size = jnp.where(inside, table[sizes + jnp.clip(far, 0, sectors - 1)], 0)
    live_sizes = (table[sizes + 2 * blk], table[sizes + 2 * blk + 1], far_size)
    psi_copy.wait()
    halo_copy.wait()
    for slot, live_size in enumerate(live_sizes):
        live = jnp.where(reach < live_size, 1.0, 0.0).astype(BF16)
        for v in range(2):
            block = psis[v, slot] if slot < 2 else halos[v]
            src[slot, :, v * size : (v + 1) * size] = block * live
    source_copy = pltpu.make_async_copy(src, sources, more.at[2])
    outs = []
    for k in range(early):
        if k == 0:
            wait_for(copies)
        terms_k = product(slot_of(core, table[SHIFTS + k]), src, lefts.at[k], rights.at[k])
        for v in range(2):
            made[k, v] = terms_k[v]
            outs.append(
                pltpu.make_async_copy(made.at[k, v], terms.at[k, v], out_sems.at[2 * k + v])
            )
            outs[-1].start()
        if k == 0:
            source_copy.start()
    source_copy.wait()
    for out in outs:
        out.wait()


def estimate(pairs, size):
    return pl.CostEstimate(
        flops=8 * pairs * size**3, bytes_accessed=20 * pairs * size * size, transcendentals=0
    )


def own_terms(sectors, table, psi, halo, left, right):
    pairs, _, size, _ = left.shape
    return pl.pallas_call(
        functools.partial(own_kernel, sectors),
        in_specs=[SMEM] + [HBM] * 4,
        out_specs=[HBM, HBM],
        out_shape=[
            jax.ShapeDtypeStruct((EARLY, 2, size, size), F32),
            jax.ShapeDtypeStruct((3, size, 2 * size), BF16),
        ],
        scratch_shapes=[
            pltpu.VMEM(psi.shape, BF16),
            pltpu.VMEM(halo.shape, BF16),
            pltpu.VMEM((EARLY, size, size), BF16),
            pltpu.VMEM((EARLY, size, size), BF16),
            pltpu.VMEM((EARLY, 2, size, size), F32),
            pltpu.VMEM((3, size, 2 * size), BF16),
            pltpu.SemaphoreType.DMA((2, EARLY)),
            pltpu.SemaphoreType.DMA((2 * EARLY,)),
            pltpu.SemaphoreType.DMA((3,)),
        ],
        compiler_params=pltpu.CompilerParams(vmem_limit_bytes=62_850_000),
        cost_estimate=estimate(100 * pairs, size),
        name="own_terms",
    )(table, psi, halo, left, right)


def level_of(top, head):
    return jnp.maximum(jnp.ceil(jnp.log2(jnp.maximum(top, 1e-30))), -90.0) - head


def folded(values):
    rows, columns = values.shape
    total = None
    for r in range(0, rows, 8):
        for c in range(0, columns, LANES):
            part = values[r : r + 8, c : c + LANES]
            total = part if total is None else total + part
    return total


def sigma_kernel(
    table, owner, words, own, sources, left, right, left_got, right_got, packed, norm,
    lefts, rights, owns, src, acc, sems, own_sems, more,
):
    core, chip = table[CORE], table[CHIP]
    pairs, size = left.shape[0], left.shape[2]
    early = own.shape[0]
    late = range(early, pairs)
    first_slot = slot_of(core, table[SHIFTS + early])
    source_copies = []
    for i in range(3):
        slot = lax.rem(first_slot + i, 3)
        source_copies.append(
            pltpu.make_async_copy(sources.at[slot], src.at[slot], more.at[i])
        )
    copies = loads(core, left, right, lefts, rights, sems, late)
    copies += loads(core, left_got, right_got, lefts, rights, sems, range(pairs), len(late))
    own_copies = [
        pltpu.make_async_copy(own.at[k], owns.at[k], own_sems.at[k]) for k in range(early)
    ]
    ordered = [source_copies[0], *copies[0], *source_copies[1:]]
    ordered += [copy for pair in copies[1:] for copy in pair] + own_copies
    for copy in ordered:
        copy.start()

    chips = packed.shape[0]
    chip_rows = size // chips
    parts = size // LANES
    tag = 2 * parts * chip_rows
    tagged = packed.shape[1] - tag
    line = jnp.broadcast_to(words[owner[0], 0:1, :], (8, LANES))
    first = lax.rem(chip * 2 * pairs, LANES)
    own_weight = pltpu.roll(line, LANES - first - core * pairs, 1)
    got_weight = pltpu.roll(line, LANES - first - (1 - core) * pairs, 1)
    facts = words[2 * chip + 1 - core, 1:2, :]
    spot = lax.broadcasted_iota(jnp.int32, (1, LANES), 1)
    shifts = [table[SHIFTS + k] for k in late]
    shifts += [
        jnp.sum(jnp.where(spot == 1 + k, facts, 0.0)).astype(jnp.int32) for k in range(pairs)
    ]

    weights = [own_weight[0:1, k : k + 1] for k in late]
    weights += [got_weight[0:1, k : k + 1] for k in range(pairs)]
    for i, weight in enumerate(weights):
        if i == 0:
            source_copies[0].wait()
            wait_for(copies[:1])
        if i == 1:
            wait_for([source_copies[1:]])
            wait_for(copies[1:3])
        if i == 3:
            wait_for(copies[3:])
        terms = product(slot_of(core, shifts[i]), src, lefts.at[i], rights.at[i])
        for v in range(2):
            total = weight * terms[v]
            acc[v] = total if i == 0 else acc[v] + total
    for copy in own_copies:
        copy.wait()

    tile = size // TILES
    here = chips // TILES
    row = lax.broadcasted_iota(jnp.int32, (tagged, LANES), 0)
    lane = lax.broadcasted_iota(jnp.int32, (tagged, LANES), 1)
    sums = [None] * 4
    for step in range(TILES):
        rows = slice(step * tile, (step + 1) * tile)
        top = None
        for v in range(2):
            total = acc[v, rows, :]
            for k in range(early):
                total += own_weight[0:1, k : k + 1] * owns[k, v, rows, :]
            acc[v, rows, :] = total
            psi = src[core, rows, v * size : (v + 1) * size].astype(F32)
            for i, part in ((v, folded(psi * total)), (2 + v, folded(psi * psi))):
                sums[i] = part if sums[i] is None else sums[i] + part
            high = jnp.max(jnp.abs(total), keepdims=True)
            top = high if top is None else jnp.maximum(top, high)
        level = level_of(top, 14.0)
        scale = jnp.exp2(-level)
        mark = jnp.where(row == 0, level, 0.0)
        for v in range(2):
            for j in range(here):
                chip_at = step * here + j
                for t in range(parts):
                    at = (v * parts + t) * chip_rows
                    packed[chip_at, at : at + chip_rows, :] = scale * acc[
                        v, chip_at * chip_rows : (chip_at + 1) * chip_rows, t * LANES : (t + 1) * LANES
                    ]
        for j in range(here):
            packed[step * here + j, tag:, :] = mark

    cross = [jnp.sum(sums[v], keepdims=True) for v in range(2)]
    level = level_of(jnp.maximum(jnp.abs(cross[0]), jnp.abs(cross[1])), 0.0)
    values = [level]
    rest = [value * jnp.exp2(-level) * HEAD for value in cross]
    for _ in range(3):
        heads = [jnp.round(value) for value in rest]
        values += heads
        rest = [(value - head) * PIECE for value, head in zip(rest, heads)]
    tags = jnp.zeros((tagged, LANES), F32)
    for i, value in enumerate(values):
        tags = jnp.where((row == 0) & (lane == i + 1), value, tags)
    for j in range(chips):
        packed[j, tag:, :] = jnp.where(lane == 0, packed[j, tag:, :], tags)
    for v in range(2):
        norm[v : v + 1, :] = jnp.broadcast_to(jnp.sum(sums[2 + v], keepdims=True), (1, LANES))


def sigma_blocks(chips, table, owner, words, own, sources, left, right, left_got, right_got):
    pairs, _, size, _ = left.shape
    lines = -(-(2 * size * size // chips // LANES + 1) // 8) * 8
    return pl.pallas_call(
        sigma_kernel,
        in_specs=[SMEM] * 2 + [VMEM] + [HBM] * 6,
        out_specs=[VMEM, VMEM],
        out_shape=[
            jax.ShapeDtypeStruct((chips, lines, LANES), F32),
            jax.ShapeDtypeStruct((2, LANES), F32),
        ],
        scratch_shapes=[
            pltpu.VMEM((2 * pairs - EARLY, size, size), BF16),
            pltpu.VMEM((2 * pairs - EARLY, size, size), BF16),
            pltpu.VMEM((EARLY, 2, size, size), F32),
            pltpu.VMEM((3, size, 2 * size), BF16),
            pltpu.VMEM((2, size, size), F32),
            pltpu.SemaphoreType.DMA((2, 2 * pairs - EARLY)),
            pltpu.SemaphoreType.DMA((EARLY,)),
            pltpu.SemaphoreType.DMA((3,)),
        ],
        compiler_params=pltpu.CompilerParams(vmem_limit_bytes=55_000_000),
        cost_estimate=estimate(pairs, size),
        name="sigma_blocks",
    )(table, owner, words, own, sources, left, right, left_got, right_got)


def on_device(
    wavefunction, left_ops, right_ops, shifts, sector_sizes, site_coef, site_energy, site_owner
):
    size = wavefunction.shape[2]
    pairs = left_ops.shape[0]
    chips, blks = lax.axis_size("chip"), lax.axis_size("blk")
    chip, core, blk = lax.axis_index("chip"), lax.axis_index("core"), lax.axis_index("blk")
    chip_rows = size // chips
    rows = chip_rows // 2
    parts = size // LANES
    words, edge, table = prepared(
        2 * chips, site_coef, site_energy[None], shifts, sector_sizes, wavefunction
    )

    swap = [(0, 1), (1, 0)]
    halo_path = [(x, x + 1) for x in range(blks - 1)] + [
        (blks + x + 1, blks + x) for x in range(blks - 1)
    ]
    halo = lax.ppermute(edge, ("core", "blk"), halo_path)
    words = lax.all_to_all(words, OP, 0, 0, tiled=True)
    left_got = lax.ppermute(left_ops, "core", swap)
    right_got = lax.ppermute(right_ops, "core", swap)
    own, sources = own_terms(
        sector_sizes.shape[0],
        table,
        wavefunction,
        halo,
        left_ops,
        right_ops,
    )
    packed, norm = sigma_blocks(
        chips,
        table,
        site_owner,
        words,
        own,
        sources,
        left_ops,
        right_ops,
        left_got,
        right_got,
    )

    blocks = lax.all_to_all(packed.astype(F16), "chip", 0, 0, tiled=True)
    tag = 2 * parts * chip_rows
    tags = blocks[:, tag, :8].astype(F32)
    cross = jnp.sum(
        (tags[:, 2:4] + (tags[:, 4:6] + tags[:, 6:8] / PIECE) / PIECE)
        / HEAD
        * jnp.exp2(tags[:, 1:2]),
        axis=0,
    )
    summed = jnp.sum(blocks[:, :tag].astype(F32) * jnp.exp2(tags[:, 0])[:, None, None], axis=0)

    halves = summed.reshape(2 * parts, 2, rows, LANES).transpose(1, 0, 2, 3)
    halves = halves.reshape(2, 1, 2 * parts * rows, LANES)
    halves = jnp.broadcast_to(halves, (2, blks) + halves.shape[2:])
    sums = jnp.pad(jnp.concatenate([cross, norm[:, 0]]), (0, LANES - 4))
    sums = jnp.broadcast_to(sums[None, None, None], (2, blks, 1, LANES))
    sent = jnp.concatenate([halves, sums], axis=2).reshape(2 * blks, -1, LANES)
    came = lax.all_to_all(sent, ("core", "blk"), 0, 0, tiled=True)
    sums = jnp.sum(came[:, -1, :4], axis=0)
    energy = lax.dynamic_index_in_dim(words[:, 1, 0], site_owner[0], 0, keepdims=False)
    cross_sum, norm_sum = sums[:2], sums[2:]
    rayleigh = (cross_sum + energy * norm_sum) / (norm_sum + 1e-06)
    ours = lax.dynamic_index_in_dim(came.reshape(2, blks, -1, LANES), blk, 1, keepdims=False)
    ours = ours[:, :-1].reshape(2, 2, parts, rows, LANES).transpose(3, 1, 0, 2, 4)
    ours = ours.reshape(rows, 2, 2, size)

    first = (chip * 2 + core) * rows
    own_sizes = lax.dynamic_slice_in_dim(sector_sizes, 2 * blk, 2, 0)[:, None]
    row_ids = (first + jnp.arange(rows, dtype=jnp.int32))[:, None, None, None]
    col_ids = jnp.arange(size, dtype=jnp.int32)
    live = (row_ids < own_sizes) & (col_ids < own_sizes)
    psi_rows = lax.dynamic_slice_in_dim(wavefunction, first, rows, 2)
    psi_rows = psi_rows.transpose(2, 0, 1, 3).astype(F32)
    value = ours + (energy - rayleigh)[None, :, None, None] * psi_rows
    return jnp.where(live, value, 0.0), rayleigh


def solution(mesh):
    ops, blks = mesh.devices.shape
    split = Mesh(mesh.devices.reshape(ops // 2, 2, blks), OP + ("blk",))
    return jax.shard_map(
        on_device,
        mesh=split,
        in_specs=(
            P(None, "blk", None, None),
            P(OP, "blk", None, None),
            P(OP, "blk", None, None),
            P(OP),
            P(),
            P(OP, None),
            P(OP),
            P(),
        ),
        out_specs=(P(OP, None, "blk", None), P()),
        check_vma=False,
    )
```

```python
import functools

import jax
import jax.numpy as jnp
from jax import lax
from jax.experimental import pallas as pl
from jax.experimental.pallas import tpu as pltpu
from jax.sharding import Mesh, PartitionSpec as P

F32, F16, BF16 = jnp.float32, jnp.float16, jnp.bfloat16
OP = ("chip", "core")
HEAD, PIECE = 1024.0, 2048.0
TILES = 4
EARLY = 2
LANES = 128
SMEM = pl.BlockSpec(memory_space=pltpu.SMEM)
VMEM = pl.BlockSpec(memory_space=pltpu.VMEM)
HBM = pl.BlockSpec(memory_space=pltpu.HBM)
CORE, BLK, CHIP, SHIFTS = 0, 1, 2, 3


def prep_kernel(coef, energy, shifts, sizes, psi, words, edge, table, sems):
    core = lax.axis_index("core")
    copies = [
        pltpu.make_async_copy(psi.at[v, 1 - core], edge.at[v], sems.at[v]) for v in range(2)
    ]
    for copy in copies:
        copy.start()
    table[CORE] = core
    table[BLK] = lax.axis_index("blk")
    table[CHIP] = lax.axis_index("chip")
    pairs, sectors = shifts.shape[0], sizes.shape[0]
    for k in range(pairs):
        table[SHIFTS + k] = shifts[k]
    for b in range(sectors):
        table[SHIFTS + pairs + b] = sizes[b]
    spot = lax.broadcasted_iota(jnp.int32, (2, LANES), 1)
    row = lax.broadcasted_iota(jnp.int32, (2, LANES), 0)
    facts = jnp.where(spot == 0, energy[0:1, 0:1], 0.0)
    for k in range(pairs):
        facts = jnp.where(spot == 1 + k, shifts[k].astype(F32), facts)
    lines = coef.shape[1] // LANES
    each = words.shape[0] // lines
    for i in range(lines):
        line = jnp.broadcast_to(coef[0:1, i * LANES : (i + 1) * LANES], (2, LANES))
        block = jnp.where(row == 0, line, facts)
        words[i * each : (i + 1) * each] = jnp.broadcast_to(block[None], (each, 2, LANES))
    for copy in copies:
        copy.wait()


def prepared(ops, coef, energy, shifts, sizes, psi):
    size = psi.shape[2]
    return pl.pallas_call(
        prep_kernel,
        in_specs=[VMEM] * 2 + [SMEM] * 2 + [HBM],
        out_specs=[VMEM, VMEM, SMEM],
        out_shape=[
            jax.ShapeDtypeStruct((ops, 2, LANES), F32),
            jax.ShapeDtypeStruct((2, size, size), BF16),
            jax.ShapeDtypeStruct((SHIFTS + shifts.shape[0] + sizes.shape[0],), jnp.int32),
        ],
        scratch_shapes=[pltpu.SemaphoreType.DMA((2,))],
        compiler_params=pltpu.CompilerParams(vmem_limit_bytes=60_000_000),
        name="prepared",
    )(coef, energy, shifts, sizes, psi)


def loads(core, left, right, lefts, rights, sems, pairs, at=0):
    return [
        (
            pltpu.make_async_copy(left.at[k, core], lefts.at[at + i], sems.at[0, at + i]),
            pltpu.make_async_copy(right.at[k, core], rights.at[at + i], sems.at[1, at + i]),
        )
        for i, k in enumerate(pairs)
    ]


def slot_of(core, shift):
    slot = core - shift
    return jnp.where((slot == 0) | (slot == 1), slot, 2)


def product(slot, src, left, right):
    size = left.shape[0]
    part = jnp.dot(left[...], src[slot], preferred_element_type=F32).astype(BF16)
    part = jnp.concatenate([part[:, :size], part[:, size:]], axis=0)
    terms = lax.dot_general(
        part, right[...], (((1,), (1,)), ((), ())), preferred_element_type=F32
    )
    return [terms[:size], terms[size:]]


def wait_for(pairs):
    for copies in pairs:
        for copy in copies:
            copy.wait()


def own_kernel(
    sectors, table, psi, halo, left, right, terms, sources,
    psis, halos, lefts, rights, made, src, sems, out_sems, more,
):
    core, blk = table[CORE], table[BLK]
    early, size = lefts.shape[0], lefts.shape[1]
    pairs = left.shape[0]
    psi_copy = pltpu.make_async_copy(psi, psis, more.at[0])
    halo_copy = pltpu.make_async_copy(halo, halos, more.at[1])
    psi_copy.start()
    halo_copy.start()
    copies = loads(core, left, right, lefts, rights, sems, range(early))
    for pair in copies:
        for copy in pair:
            copy.start()
    row = lax.broadcasted_iota(jnp.int32, (size, size), 0)
    col = lax.broadcasted_iota(jnp.int32, (size, size), 1)
    reach = jnp.maximum(row, col)
    sizes = SHIFTS + pairs
    far = 2 * blk - 1 + 3 * core
    inside = (far >= 0) & (far < sectors)
    far_size = jnp.where(inside, table[sizes + jnp.clip(far, 0, sectors - 1)], 0)
    live_sizes = (table[sizes + 2 * blk], table[sizes + 2 * blk + 1], far_size)
    psi_copy.wait()
    halo_copy.wait()
    for slot, live_size in enumerate(live_sizes):
        live = jnp.where(reach < live_size, 1.0, 0.0).astype(BF16)
        for v in range(2):
            block = psis[v, slot] if slot < 2 else halos[v]
            src[slot, :, v * size : (v + 1) * size] = block * live
    source_copy = pltpu.make_async_copy(src, sources, more.at[2])
    outs = []
    for k in range(early):
        if k == 0:
            wait_for(copies)
        terms_k = product(slot_of(core, table[SHIFTS + k]), src, lefts.at[k], rights.at[k])
        for v in range(2):
            made[k, v] = terms_k[v]
            outs.append(
                pltpu.make_async_copy(made.at[k, v], terms.at[k, v], out_sems.at[2 * k + v])
            )
            outs[-1].start()
        if k == 0:
            source_copy.start()
    source_copy.wait()
    for out in outs:
        out.wait()


def estimate(pairs, size):
    return pl.CostEstimate(
        flops=8 * pairs * size**3, bytes_accessed=20 * pairs * size * size, transcendentals=0
    )


def own_terms(sectors, table, psi, halo, left, right):
    pairs, _, size, _ = left.shape
    return pl.pallas_call(
        functools.partial(own_kernel, sectors),
        in_specs=[SMEM] + [HBM] * 4,
        out_specs=[HBM, HBM],
        out_shape=[
            jax.ShapeDtypeStruct((EARLY, 2, size, size), F32),
            jax.ShapeDtypeStruct((3, size, 2 * size), BF16),
        ],
        scratch_shapes=[
            pltpu.VMEM(psi.shape, BF16),
            pltpu.VMEM(halo.shape, BF16),
            pltpu.VMEM((EARLY, size, size), BF16),
            pltpu.VMEM((EARLY, size, size), BF16),
            pltpu.VMEM((EARLY, 2, size, size), F32),
            pltpu.VMEM((3, size, 2 * size), BF16),
            pltpu.SemaphoreType.DMA((2, EARLY)),
            pltpu.SemaphoreType.DMA((2 * EARLY,)),
            pltpu.SemaphoreType.DMA((3,)),
        ],
        compiler_params=pltpu.CompilerParams(vmem_limit_bytes=62_850_000),
        cost_estimate=estimate(100 * pairs, size),
        name="own_terms",
    )(table, psi, halo, left, right)


def level_of(top, head):
    return jnp.maximum(jnp.ceil(jnp.log2(jnp.maximum(top, 1e-30))), -90.0) - head


def folded(values):
    rows, columns = values.shape
    total = None
    for r in range(0, rows, 8):
        for c in range(0, columns, LANES):
            part = values[r : r + 8, c : c + LANES]
            total = part if total is None else total + part
    return total


def sigma_kernel(
    table, owner, words, own, sources, left, right, left_got, right_got, packed, norm,
    lefts, rights, owns, src, acc, sems, own_sems, more,
):
    core, chip = table[CORE], table[CHIP]
    pairs, size = left.shape[0], left.shape[2]
    early = own.shape[0]
    late = range(early, pairs)
    first_slot = slot_of(core, table[SHIFTS + early])
    source_copies = []
    for i in range(3):
        slot = lax.rem(first_slot + i, 3)
        source_copies.append(
            pltpu.make_async_copy(sources.at[slot], src.at[slot], more.at[i])
        )
    copies = loads(core, left, right, lefts, rights, sems, late)
    copies += loads(core, left_got, right_got, lefts, rights, sems, range(pairs), len(late))
    own_copies = [
        pltpu.make_async_copy(own.at[k], owns.at[k], own_sems.at[k]) for k in range(early)
    ]
    ordered = [source_copies[0], *copies[0], *source_copies[1:]]
    ordered += [copy for pair in copies[1:] for copy in pair] + own_copies
    for copy in ordered:
        copy.start()

    chips = packed.shape[0]
    chip_rows = size // chips
    parts = size // LANES
    tag = 2 * parts * chip_rows
    tagged = packed.shape[1] - tag
    line = jnp.broadcast_to(words[owner[0], 0:1, :], (8, LANES))
    first = lax.rem(chip * 2 * pairs, LANES)
    own_weight = pltpu.roll(line, LANES - first - core * pairs, 1)
    got_weight = pltpu.roll(line, LANES - first - (1 - core) * pairs, 1)
    facts = words[2 * chip + 1 - core, 1:2, :]
    spot = lax.broadcasted_iota(jnp.int32, (1, LANES), 1)
    shifts = [table[SHIFTS + k] for k in late]
    shifts += [
        jnp.sum(jnp.where(spot == 1 + k, facts, 0.0)).astype(jnp.int32) for k in range(pairs)
    ]

    weights = [own_weight[0:1, k : k + 1] for k in late]
    weights += [got_weight[0:1, k : k + 1] for k in range(pairs)]
    for i, weight in enumerate(weights):
        if i == 0:
            source_copies[0].wait()
            wait_for(copies[:1])
        if i == 1:
            wait_for([source_copies[1:]])
            wait_for(copies[1:3])
        if i == 3:
            wait_for(copies[3:])
        terms = product(slot_of(core, shifts[i]), src, lefts.at[i], rights.at[i])
        for v in range(2):
            total = weight * terms[v]
            acc[v] = total if i == 0 else acc[v] + total
    for copy in own_copies:
        copy.wait()

    tile = size // TILES
    here = chips // TILES
    row = lax.broadcasted_iota(jnp.int32, (tagged, LANES), 0)
    lane = lax.broadcasted_iota(jnp.int32, (tagged, LANES), 1)
    sums = [None] * 4
    for step in range(TILES):
        rows = slice(step * tile, (step + 1) * tile)
        top = None
        for v in range(2):
            total = acc[v, rows, :]
            for k in range(early):
                total += own_weight[0:1, k : k + 1] * owns[k, v, rows, :]
            acc[v, rows, :] = total
            psi = src[core, rows, v * size : (v + 1) * size].astype(F32)
            for i, part in ((v, folded(psi * total)), (2 + v, folded(psi * psi))):
                sums[i] = part if sums[i] is None else sums[i] + part
            high = jnp.max(jnp.abs(total), keepdims=True)
            top = high if top is None else jnp.maximum(top, high)
        level = level_of(top, 14.0)
        scale = jnp.exp2(-level)
        mark = jnp.where(row == 0, level, 0.0)
        for v in range(2):
            for j in range(here):
                chip_at = step * here + j
                for t in range(parts):
                    at = (v * parts + t) * chip_rows
                    packed[chip_at, at : at + chip_rows, :] = scale * acc[
                        v, chip_at * chip_rows : (chip_at + 1) * chip_rows, t * LANES : (t + 1) * LANES
                    ]
        for j in range(here):
            packed[step * here + j, tag:, :] = mark

    cross = [jnp.sum(sums[v], keepdims=True) for v in range(2)]
    level = level_of(jnp.maximum(jnp.abs(cross[0]), jnp.abs(cross[1])), 0.0)
    values = [level]
    rest = [value * jnp.exp2(-level) * HEAD for value in cross]
    for _ in range(3):
        heads = [jnp.round(value) for value in rest]
        values += heads
        rest = [(value - head) * PIECE for value, head in zip(rest, heads)]
    tags = jnp.zeros((tagged, LANES), F32)
    for i, value in enumerate(values):
        tags = jnp.where((row == 0) & (lane == i + 1), value, tags)
    for j in range(chips):
        packed[j, tag:, :] = jnp.where(lane == 0, packed[j, tag:, :], tags)
    for v in range(2):
        norm[v : v + 1, :] = jnp.broadcast_to(jnp.sum(sums[2 + v], keepdims=True), (1, LANES))


def sigma_blocks(chips, table, owner, words, own, sources, left, right, left_got, right_got):
    pairs, _, size, _ = left.shape
    lines = -(-(2 * size * size // chips // LANES + 1) // 8) * 8
    return pl.pallas_call(
        sigma_kernel,
        in_specs=[SMEM] * 2 + [VMEM] + [HBM] * 6,
        out_specs=[VMEM, VMEM],
        out_shape=[
            jax.ShapeDtypeStruct((chips, lines, LANES), F32),
            jax.ShapeDtypeStruct((2, LANES), F32),
        ],
        scratch_shapes=[
            pltpu.VMEM((2 * pairs - EARLY, size, size), BF16),
            pltpu.VMEM((2 * pairs - EARLY, size, size), BF16),
            pltpu.VMEM((EARLY, 2, size, size), F32),
            pltpu.VMEM((3, size, 2 * size), BF16),
            pltpu.VMEM((2, size, size), F32),
            pltpu.SemaphoreType.DMA((2, 2 * pairs - EARLY)),
            pltpu.SemaphoreType.DMA((EARLY,)),
            pltpu.SemaphoreType.DMA((3,)),
        ],
        compiler_params=pltpu.CompilerParams(vmem_limit_bytes=55_000_000),
        cost_estimate=estimate(pairs, size),
        name="sigma_blocks",
    )(table, owner, words, own, sources, left, right, left_got, right_got)


def finish_kernel(came, energy, psi, live, residual, rayleigh):
    blk = lax.axis_index("blk")
    blks = came.shape[0] // 2
    rows, size = psi.shape[0], psi.shape[3]
    parts = size // LANES
    sums = jnp.sum(came[:, came.shape[1] - 1, :], axis=0, keepdims=True)
    for v in range(2):
        norm = sums[:, 2 + v : 3 + v]
        quotient = (sums[:, v : v + 1] + energy[...] * norm) / (norm + 1e-06)
        rayleigh[v] = jnp.sum(quotient)
        factor = energy[...] - quotient
        for q in range(rows):
            for b in range(2):
                for t in range(parts):
                    at = (v * parts + t) * rows + q
                    lanes = slice(t * LANES, (t + 1) * LANES)
                    value = came[b * blks + blk, at : at + 1, :]
                    value = value + factor * psi[q, v, b : b + 1, lanes]
                    residual[q, v, b : b + 1, lanes] = jnp.where(
                        live[q, b : b + 1, lanes] > 0.0, value, 0.0
                    )


def finished(came, energy, psi, live):
    return pl.pallas_call(
        finish_kernel,
        in_specs=[VMEM] * 4,
        out_specs=[VMEM, SMEM],
        out_shape=[
            jax.ShapeDtypeStruct(psi.shape, F32),
            jax.ShapeDtypeStruct((2,), F32),
        ],
        compiler_params=pltpu.CompilerParams(vmem_limit_bytes=16 * 1024 * 1024),
        name="finished",
    )(came, energy, psi, live)


def on_device(
    wavefunction, left_ops, right_ops, shifts, sector_sizes, site_coef, site_energy, site_owner
):
    size = wavefunction.shape[2]
    pairs = left_ops.shape[0]
    chips, blks = lax.axis_size("chip"), lax.axis_size("blk")
    chip, core, blk = lax.axis_index("chip"), lax.axis_index("core"), lax.axis_index("blk")
    chip_rows = size // chips
    rows = chip_rows // 2
    parts = size // LANES
    words, edge, table = prepared(
        2 * chips, site_coef, site_energy[None], shifts, sector_sizes, wavefunction
    )

    swap = [(0, 1), (1, 0)]
    halo_path = [(x, x + 1) for x in range(blks - 1)] + [
        (blks + x + 1, blks + x) for x in range(blks - 1)
    ]
    halo = lax.ppermute(edge, ("core", "blk"), halo_path)
    words = lax.all_to_all(words, OP, 0, 0, tiled=True)
    left_got = lax.ppermute(left_ops, "core", swap)
    right_got = lax.ppermute(right_ops, "core", swap)
    own, sources = own_terms(
        sector_sizes.shape[0],
        table,
        wavefunction,
        halo,
        left_ops,
        right_ops,
    )
    packed, norm = sigma_blocks(
        chips,
        table,
        site_owner,
        words,
        own,
        sources,
        left_ops,
        right_ops,
        left_got,
        right_got,
    )

    blocks = lax.all_to_all(packed.astype(F16), "chip", 0, 0, tiled=True)
    tag = 2 * parts * chip_rows
    tags = blocks[:, tag, :8].astype(F32)
    cross = jnp.sum(
        (tags[:, 2:4] + (tags[:, 4:6] + tags[:, 6:8] / PIECE) / PIECE)
        / HEAD
        * jnp.exp2(tags[:, 1:2]),
        axis=0,
    )
    summed = jnp.sum(blocks[:, :tag].astype(F32) * jnp.exp2(tags[:, 0])[:, None, None], axis=0)

    halves = summed.reshape(2 * parts, 2, rows, LANES).transpose(1, 0, 2, 3)
    halves = halves.reshape(2, 1, 2 * parts * rows, LANES)
    halves = jnp.broadcast_to(halves, (2, blks) + halves.shape[2:])
    sums = jnp.pad(jnp.concatenate([cross, norm[:, 0]]), (0, LANES - 4))
    sums = jnp.broadcast_to(sums[None, None, None], (2, blks, 1, LANES))
    sent = jnp.concatenate([halves, sums], axis=2).reshape(2 * blks, -1, LANES)
    came = lax.all_to_all(sent, ("core", "blk"), 0, 0, tiled=True)
    energy = lax.dynamic_index_in_dim(words[:, 1, 0], site_owner[0], 0, keepdims=False)

    first = (chip * 2 + core) * rows
    own_sizes = lax.dynamic_slice_in_dim(sector_sizes, 2 * blk, 2, 0)[:, None]
    row_ids = (first + jnp.arange(rows, dtype=jnp.int32))[:, None, None, None]
    col_ids = jnp.arange(size, dtype=jnp.int32)
    live = ((row_ids < own_sizes) & (col_ids < own_sizes))[:, 0].astype(F32)
    psi_rows = lax.dynamic_slice_in_dim(wavefunction, first, rows, 2)
    psi_rows = psi_rows.transpose(2, 0, 1, 3).astype(F32)
    residual, rayleigh = finished(came, energy.reshape(1, 1), psi_rows, live)
    return residual, rayleigh


def solution(mesh):
    ops, blks = mesh.devices.shape
    split = Mesh(mesh.devices.reshape(ops // 2, 2, blks), OP + ("blk",))
    return jax.shard_map(
        on_device,
        mesh=split,
        in_specs=(
            P(None, "blk", None, None),
            P(OP, "blk", None, None),
            P(OP, "blk", None, None),
            P(OP),
            P(),
            P(OP, None),
            P(OP),
            P(),
        ),
        out_specs=(P(OP, None, "blk", None), P()),
        check_vma=False,
    )
```

```python
import functools

import jax
import jax.numpy as jnp
from jax import lax
from jax.experimental import pallas as pl
from jax.experimental.pallas import tpu as pltpu
from jax.sharding import Mesh, PartitionSpec as P

F32, F16, BF16 = jnp.float32, jnp.float16, jnp.bfloat16
OP = ("chip", "core")
HEAD, PIECE = 1024.0, 2048.0
TILES = 4
EARLY = 2
LANES = 128
SMEM = pl.BlockSpec(memory_space=pltpu.SMEM)
VMEM = pl.BlockSpec(memory_space=pltpu.VMEM)
HBM = pl.BlockSpec(memory_space=pltpu.HBM)
CORE, BLK, CHIP, SHIFTS = 0, 1, 2, 3


def prep_kernel(
    coef, energy, shifts, sizes, psi, words, edge, table, made, held, sems, out_sems
):
    core = lax.axis_index("core")
    copies = [
        pltpu.make_async_copy(psi.at[v, 1 - core], held.at[v], sems.at[v]) for v in range(2)
    ]
    for copy in copies:
        copy.start()
    table[CORE] = core
    table[BLK] = lax.axis_index("blk")
    table[CHIP] = lax.axis_index("chip")
    pairs, sectors = shifts.shape[0], sizes.shape[0]
    for k in range(pairs):
        table[SHIFTS + k] = shifts[k]
    for b in range(sectors):
        table[SHIFTS + pairs + b] = sizes[b]
    spot = lax.broadcasted_iota(jnp.int32, (2, LANES), 1)
    row = lax.broadcasted_iota(jnp.int32, (2, LANES), 0)
    facts = jnp.where(spot == 0, energy[0:1, 0:1], 0.0)
    for k in range(pairs):
        facts = jnp.where(spot == 1 + k, shifts[k].astype(F32), facts)
    lines = coef.shape[1] // LANES
    each = words.shape[0] // lines
    for i in range(lines):
        line = jnp.broadcast_to(coef[0:1, i * LANES : (i + 1) * LANES], (2, LANES))
        block = jnp.where(row == 0, line, facts)
        made[i * each : (i + 1) * each] = jnp.broadcast_to(block[None], (each, 2, LANES))
    outs = [pltpu.make_async_copy(made, words, out_sems.at[2])]
    outs[0].start()
    for v in range(2):
        copies[v].wait()
        outs.append(pltpu.make_async_copy(held.at[v], edge.at[v], out_sems.at[v]))
        outs[-1].start()
    for out in outs:
        out.wait()


def prepared(ops, coef, energy, shifts, sizes, psi):
    size = psi.shape[2]
    return pl.pallas_call(
        prep_kernel,
        in_specs=[VMEM] * 2 + [SMEM] * 2 + [HBM],
        out_specs=[HBM, HBM, SMEM],
        out_shape=[
            jax.ShapeDtypeStruct((ops, 2, LANES), F32),
            jax.ShapeDtypeStruct((2, size, size), BF16),
            jax.ShapeDtypeStruct((SHIFTS + shifts.shape[0] + sizes.shape[0],), jnp.int32),
        ],
        scratch_shapes=[
            pltpu.VMEM((ops, 2, LANES), F32),
            pltpu.VMEM((2, size, size), BF16),
            pltpu.SemaphoreType.DMA((2,)),
            pltpu.SemaphoreType.DMA((3,)),
        ],
        compiler_params=pltpu.CompilerParams(vmem_limit_bytes=60_000_000),
        name="prepared",
    )(coef, energy, shifts, sizes, psi)


def loads(core, left, right, lefts, rights, sems, pairs, at=0):
    return [
        (
            pltpu.make_async_copy(left.at[k, core], lefts.at[at + i], sems.at[0, at + i]),
            pltpu.make_async_copy(right.at[k, core], rights.at[at + i], sems.at[1, at + i]),
        )
        for i, k in enumerate(pairs)
    ]


def slot_of(core, shift):
    slot = core - shift
    return jnp.where((slot == 0) | (slot == 1), slot, 2)


def product(slot, src, left, right):
    size = left.shape[0]
    part = jnp.dot(left[...], src[slot], preferred_element_type=F32).astype(BF16)
    part = jnp.concatenate([part[:, :size], part[:, size:]], axis=0)
    terms = lax.dot_general(
        part, right[...], (((1,), (1,)), ((), ())), preferred_element_type=F32
    )
    return [terms[:size], terms[size:]]


def wait_for(pairs):
    for copies in pairs:
        for copy in copies:
            copy.wait()


def own_kernel(
    sectors, table, psi, halo, left, right, terms, sources,
    psis, halos, lefts, rights, made, src, sems, out_sems, more,
):
    core, blk = table[CORE], table[BLK]
    early, size = lefts.shape[0], lefts.shape[1]
    pairs = left.shape[0]
    psi_copy = pltpu.make_async_copy(psi, psis, more.at[0])
    halo_copy = pltpu.make_async_copy(halo, halos, more.at[1])
    psi_copy.start()
    halo_copy.start()
    copies = loads(core, left, right, lefts, rights, sems, range(early))
    for pair in copies:
        for copy in pair:
            copy.start()
    row = lax.broadcasted_iota(jnp.int32, (size, size), 0)
    col = lax.broadcasted_iota(jnp.int32, (size, size), 1)
    reach = jnp.maximum(row, col)
    sizes = SHIFTS + pairs
    far = 2 * blk - 1 + 3 * core
    inside = (far >= 0) & (far < sectors)
    far_size = jnp.where(inside, table[sizes + jnp.clip(far, 0, sectors - 1)], 0)
    live_sizes = (table[sizes + 2 * blk], table[sizes + 2 * blk + 1], far_size)
    psi_copy.wait()
    halo_copy.wait()
    for slot, live_size in enumerate(live_sizes):
        live = jnp.where(reach < live_size, 1.0, 0.0).astype(BF16)
        for v in range(2):
            block = psis[v, slot] if slot < 2 else halos[v]
            src[slot, :, v * size : (v + 1) * size] = block * live
    source_copy = pltpu.make_async_copy(src, sources, more.at[2])
    outs = []
    for k in range(early):
        if k == 0:
            wait_for(copies)
        terms_k = product(slot_of(core, table[SHIFTS + k]), src, lefts.at[k], rights.at[k])
        for v in range(2):
            made[k, v] = terms_k[v]
            outs.append(
                pltpu.make_async_copy(made.at[k, v], terms.at[k, v], out_sems.at[2 * k + v])
            )
            outs[-1].start()
        if k == 0:
            source_copy.start()
    source_copy.wait()
    for out in outs:
        out.wait()


def estimate(pairs, size):
    return pl.CostEstimate(
        flops=8 * pairs * size**3, bytes_accessed=20 * pairs * size * size, transcendentals=0
    )


def own_terms(sectors, table, psi, halo, left, right):
    pairs, _, size, _ = left.shape
    return pl.pallas_call(
        functools.partial(own_kernel, sectors),
        in_specs=[SMEM] + [HBM] * 4,
        out_specs=[HBM, HBM],
        out_shape=[
            jax.ShapeDtypeStruct((EARLY, 2, size, size), F32),
            jax.ShapeDtypeStruct((3, size, 2 * size), BF16),
        ],
        scratch_shapes=[
            pltpu.VMEM(psi.shape, BF16),
            pltpu.VMEM(halo.shape, BF16),
            pltpu.VMEM((EARLY, size, size), BF16),
            pltpu.VMEM((EARLY, size, size), BF16),
            pltpu.VMEM((EARLY, 2, size, size), F32),
            pltpu.VMEM((3, size, 2 * size), BF16),
            pltpu.SemaphoreType.DMA((2, EARLY)),
            pltpu.SemaphoreType.DMA((2 * EARLY,)),
            pltpu.SemaphoreType.DMA((3,)),
        ],
        compiler_params=pltpu.CompilerParams(vmem_limit_bytes=62_850_000),
        cost_estimate=estimate(100 * pairs, size),
        name="own_terms",
    )(table, psi, halo, left, right)


def level_of(top, head):
    return jnp.maximum(jnp.ceil(jnp.log2(jnp.maximum(top, 1e-30))), -90.0) - head


def folded(values):
    rows, columns = values.shape
    total = None
    for r in range(0, rows, 8):
        for c in range(0, columns, LANES):
            part = values[r : r + 8, c : c + LANES]
            total = part if total is None else total + part
    return total


def sigma_kernel(
    table, owner, words, own, sources, left, right, left_got, right_got, packed, norm,
    lefts, rights, owns, src, acc, sems, own_sems, more,
):
    core, chip = table[CORE], table[CHIP]
    pairs, size = left.shape[0], left.shape[2]
    early = own.shape[0]
    late = range(early, pairs)
    first_slot = slot_of(core, table[SHIFTS + early])
    source_copies = []
    for i in range(3):
        slot = lax.rem(first_slot + i, 3)
        source_copies.append(
            pltpu.make_async_copy(sources.at[slot], src.at[slot], more.at[i])
        )
    copies = loads(core, left, right, lefts, rights, sems, late)
    copies += loads(core, left_got, right_got, lefts, rights, sems, range(pairs), len(late))
    own_copies = [
        pltpu.make_async_copy(own.at[k], owns.at[k], own_sems.at[k]) for k in range(early)
    ]
    ordered = [source_copies[0], *copies[0], *source_copies[1:]]
    ordered += [copy for pair in copies[1:] for copy in pair] + own_copies
    for copy in ordered:
        copy.start()

    chips = packed.shape[0]
    chip_rows = size // chips
    parts = size // LANES
    tag = 2 * parts * chip_rows
    tagged = packed.shape[1] - tag
    line = jnp.broadcast_to(words[owner[0], 0:1, :], (8, LANES))
    first = lax.rem(chip * 2 * pairs, LANES)
    own_weight = pltpu.roll(line, LANES - first - core * pairs, 1)
    got_weight = pltpu.roll(line, LANES - first - (1 - core) * pairs, 1)
    facts = words[2 * chip + 1 - core, 1:2, :]
    spot = lax.broadcasted_iota(jnp.int32, (1, LANES), 1)
    shifts = [table[SHIFTS + k] for k in late]
    shifts += [
        jnp.sum(jnp.where(spot == 1 + k, facts, 0.0)).astype(jnp.int32) for k in range(pairs)
    ]

    weights = [own_weight[0:1, k : k + 1] for k in late]
    weights += [got_weight[0:1, k : k + 1] for k in range(pairs)]
    for i, weight in enumerate(weights):
        if i == 0:
            source_copies[0].wait()
            wait_for(copies[:1])
        if i == 1:
            wait_for([source_copies[1:]])
            wait_for(copies[1:3])
        if i == 3:
            wait_for(copies[3:])
        terms = product(slot_of(core, shifts[i]), src, lefts.at[i], rights.at[i])
        for v in range(2):
            total = weight * terms[v]
            acc[v] = total if i == 0 else acc[v] + total
    for copy in own_copies:
        copy.wait()

    tile = size // TILES
    here = chips // TILES
    row = lax.broadcasted_iota(jnp.int32, (tagged, LANES), 0)
    lane = lax.broadcasted_iota(jnp.int32, (tagged, LANES), 1)
    sums = [None] * 4
    for step in range(TILES):
        rows = slice(step * tile, (step + 1) * tile)
        top = None
        for v in range(2):
            total = acc[v, rows, :]
            for k in range(early):
                total += own_weight[0:1, k : k + 1] * owns[k, v, rows, :]
            acc[v, rows, :] = total
            psi = src[core, rows, v * size : (v + 1) * size].astype(F32)
            for i, part in ((v, folded(psi * total)), (2 + v, folded(psi * psi))):
                sums[i] = part if sums[i] is None else sums[i] + part
            high = jnp.max(jnp.abs(total), keepdims=True)
            top = high if top is None else jnp.maximum(top, high)
        level = level_of(top, 14.0)
        scale = jnp.exp2(-level)
        mark = jnp.where(row == 0, level, 0.0)
        for v in range(2):
            for j in range(here):
                chip_at = step * here + j
                for t in range(parts):
                    at = (v * parts + t) * chip_rows
                    packed[chip_at, at : at + chip_rows, :] = scale * acc[
                        v, chip_at * chip_rows : (chip_at + 1) * chip_rows, t * LANES : (t + 1) * LANES
                    ]
        for j in range(here):
            packed[step * here + j, tag:, :] = mark

    cross = [jnp.sum(sums[v], keepdims=True) for v in range(2)]
    level = level_of(jnp.maximum(jnp.abs(cross[0]), jnp.abs(cross[1])), 0.0)
    values = [level]
    rest = [value * jnp.exp2(-level) * HEAD for value in cross]
    for _ in range(3):
        heads = [jnp.round(value) for value in rest]
        values += heads
        rest = [(value - head) * PIECE for value, head in zip(rest, heads)]
    tags = jnp.zeros((tagged, LANES), F32)
    for i, value in enumerate(values):
        tags = jnp.where((row == 0) & (lane == i + 1), value, tags)
    for j in range(chips):
        packed[j, tag:, :] = jnp.where(lane == 0, packed[j, tag:, :], tags)
    for v in range(2):
        norm[v : v + 1, :] = jnp.broadcast_to(jnp.sum(sums[2 + v], keepdims=True), (1, LANES))


def sigma_blocks(chips, table, owner, words, own, sources, left, right, left_got, right_got):
    pairs, _, size, _ = left.shape
    lines = -(-(2 * size * size // chips // LANES + 1) // 8) * 8
    return pl.pallas_call(
        sigma_kernel,
        in_specs=[SMEM] * 2 + [VMEM] + [HBM] * 6,
        out_specs=[VMEM, VMEM],
        out_shape=[
            jax.ShapeDtypeStruct((chips, lines, LANES), F32),
            jax.ShapeDtypeStruct((2, LANES), F32),
        ],
        scratch_shapes=[
            pltpu.VMEM((2 * pairs - EARLY, size, size), BF16),
            pltpu.VMEM((2 * pairs - EARLY, size, size), BF16),
            pltpu.VMEM((EARLY, 2, size, size), F32),
            pltpu.VMEM((3, size, 2 * size), BF16),
            pltpu.VMEM((2, size, size), F32),
            pltpu.SemaphoreType.DMA((2, 2 * pairs - EARLY)),
            pltpu.SemaphoreType.DMA((EARLY,)),
            pltpu.SemaphoreType.DMA((3,)),
        ],
        compiler_params=pltpu.CompilerParams(vmem_limit_bytes=55_000_000),
        cost_estimate=estimate(pairs, size),
        name="sigma_blocks",
    )(table, owner, words, own, sources, left, right, left_got, right_got)


def finish_kernel(came, energy, psi, live, residual, rayleigh):
    blk = lax.axis_index("blk")
    blks = came.shape[0] // 2
    rows, size = psi.shape[0], psi.shape[3]
    parts = size // LANES
    sums = jnp.sum(came[:, came.shape[1] - 1, :], axis=0, keepdims=True)
    for v in range(2):
        norm = sums[:, 2 + v : 3 + v]
        quotient = (sums[:, v : v + 1] + energy[...] * norm) / (norm + 1e-06)
        rayleigh[v] = jnp.sum(quotient)
        factor = energy[...] - quotient
        for q in range(rows):
            for b in range(2):
                for t in range(parts):
                    at = (v * parts + t) * rows + q
                    lanes = slice(t * LANES, (t + 1) * LANES)
                    value = came[b * blks + blk, at : at + 1, :]
                    value = value + factor * psi[q, v, b : b + 1, lanes]
                    residual[q, v, b : b + 1, lanes] = jnp.where(
                        live[q, b : b + 1, lanes] > 0.0, value, 0.0
                    )


def finished(came, energy, psi, live):
    return pl.pallas_call(
        finish_kernel,
        in_specs=[VMEM] * 4,
        out_specs=[VMEM, SMEM],
        out_shape=[
            jax.ShapeDtypeStruct(psi.shape, F32),
            jax.ShapeDtypeStruct((2,), F32),
        ],
        compiler_params=pltpu.CompilerParams(vmem_limit_bytes=16 * 1024 * 1024),
        name="finished",
    )(came, energy, psi, live)


def on_device(
    wavefunction, left_ops, right_ops, shifts, sector_sizes, site_coef, site_energy, site_owner
):
    size = wavefunction.shape[2]
    pairs = left_ops.shape[0]
    chips, blks = lax.axis_size("chip"), lax.axis_size("blk")
    chip, core, blk = lax.axis_index("chip"), lax.axis_index("core"), lax.axis_index("blk")
    chip_rows = size // chips
    rows = chip_rows // 2
    parts = size // LANES
    words, edge, table = prepared(
        2 * chips, site_coef, site_energy[None], shifts, sector_sizes, wavefunction
    )

    swap = [(0, 1), (1, 0)]
    halo_path = [(x, x + 1) for x in range(blks - 1)] + [
        (blks + x + 1, blks + x) for x in range(blks - 1)
    ]
    halo = lax.ppermute(edge, ("core", "blk"), halo_path)
    words = lax.all_to_all(words, OP, 0, 0, tiled=True)
    left_got = lax.ppermute(left_ops, "core", swap)
    right_got = lax.ppermute(right_ops, "core", swap)
    own, sources = own_terms(
        sector_sizes.shape[0],
        table,
        wavefunction,
        halo,
        left_ops,
        right_ops,
    )
    packed, norm = sigma_blocks(
        chips,
        table,
        site_owner,
        words,
        own,
        sources,
        left_ops,
        right_ops,
        left_got,
        right_got,
    )

    blocks = lax.all_to_all(packed.astype(F16), "chip", 0, 0, tiled=True)
    tag = 2 * parts * chip_rows
    tags = blocks[:, tag, :8].astype(F32)
    cross = jnp.sum(
        (tags[:, 2:4] + (tags[:, 4:6] + tags[:, 6:8] / PIECE) / PIECE)
        / HEAD
        * jnp.exp2(tags[:, 1:2]),
        axis=0,
    )
    summed = jnp.sum(blocks[:, :tag].astype(F32) * jnp.exp2(tags[:, 0])[:, None, None], axis=0)

    halves = summed.reshape(2 * parts, 2, rows, LANES).transpose(1, 0, 2, 3)
    halves = halves.reshape(2, 1, 2 * parts * rows, LANES)
    halves = jnp.broadcast_to(halves, (2, blks) + halves.shape[2:])
    sums = jnp.pad(jnp.concatenate([cross, norm[:, 0]]), (0, LANES - 4))
    sums = jnp.broadcast_to(sums[None, None, None], (2, blks, 1, LANES))
    sent = jnp.concatenate([halves, sums], axis=2).reshape(2 * blks, -1, LANES)
    came = lax.all_to_all(sent, ("core", "blk"), 0, 0, tiled=True)
    energy = lax.dynamic_index_in_dim(words[:, 1, 0], site_owner[0], 0, keepdims=False)

    first = (chip * 2 + core) * rows
    own_sizes = lax.dynamic_slice_in_dim(sector_sizes, 2 * blk, 2, 0)[:, None]
    row_ids = (first + jnp.arange(rows, dtype=jnp.int32))[:, None, None, None]
    col_ids = jnp.arange(size, dtype=jnp.int32)
    live = ((row_ids < own_sizes) & (col_ids < own_sizes))[:, 0].astype(F32)
    psi_rows = lax.dynamic_slice_in_dim(wavefunction, first, rows, 2)
    psi_rows = psi_rows.transpose(2, 0, 1, 3).astype(F32)
    residual, rayleigh = finished(came, energy.reshape(1, 1), psi_rows, live)
    return residual, rayleigh


def solution(mesh):
    ops, blks = mesh.devices.shape
    split = Mesh(mesh.devices.reshape(ops // 2, 2, blks), OP + ("blk",))
    return jax.shard_map(
        on_device,
        mesh=split,
        in_specs=(
            P(None, "blk", None, None),
            P(OP, "blk", None, None),
            P(OP, "blk", None, None),
            P(OP),
            P(),
            P(OP, None),
            P(OP),
            P(),
        ),
        out_specs=(P(OP, None, "blk", None), P()),
        check_vma=False,
    )
```
